512 devices in a mesh: wide: 64 (over z, y), narrow: 8 (over x, core).
Axes of the slice: x: 4, y: 8, z: 8, core: 2. Of those that a mesh axis runs over, the one named last changes fastest.
Arguments:
- snapshots: float32 [128, 524288], P('wide', 'narrow'), may hold values from -1000 to 1000
Outputs:
- q_scaled: float32 [524288, 128], P(('narrow', 'wide'))
- r_scaled: float32 [128, 128], replicated
The draws below stay inside these ranges and needn't reach their ends.
All inputs are finite; a program needn't handle non-finite values.
Results may differ from the reference program's by a relative error of at most 0.0003.
Values sent between devices are 32-bit elements; how exact they have to be, the bound alone decides.
No kernel may reach another device: no remote copies, remote signals or barrier semaphores. Data moves between devices by JAX's collectives and lax.ppermute only.
A program may use at most 64 MiB of HBM per device.

```python
import math
import jax
import jax.numpy as jnp

SNAPS = 128
ROWS = 524288


def draw_snapshots(key, part):
    key = jax.random.fold_in(key, 17)
    key_noise = jax.random.fold_in(key, 0)
    key_common = jax.random.fold_in(key, 1)
    key_column = jax.random.fold_in(key, 3)
    key_row = jax.random.fold_in(key, 4)
    rising = 1.0 + 2.0 * jnp.arange(ROWS, dtype=jnp.float32) / ROWS
    column_scale = jnp.exp(jax.random.uniform(key_column, (SNAPS,), jnp.float32, 0.0, math.log(10.0)))
    common = jnp.clip(jax.random.normal(key_common, (ROWS,), jnp.float32), -4.0, 4.0)
    noise = jnp.clip(jax.random.normal(key_noise, (SNAPS, ROWS), jnp.float32), -4.0, 4.0)
    shared = jnp.broadcast_to(common[None, :], (SNAPS, ROWS))
    spread = 0.5
    low_scale = 0.3
    high_scale = 3.0
    row_scale = jnp.exp(jax.random.uniform(key_row, (ROWS,), jnp.float32, math.log(low_scale), math.log(high_scale)))
    lagged = noise + 0.5 * jnp.roll(noise, 1, axis=0)
    mixed = shared + spread * lagged
    return (column_scale[:, None] * (row_scale * rising)[None, :] * mixed).astype(jnp.float32)


def setup_inputs(seed: int = 0) -> dict:
    arg_keys = jax.random.split(jax.random.key(seed), 2)
    return {
        "snapshots": draw_snapshots(jax.random.fold_in(arg_keys[1], 71), 0),
    }


def reference(snapshots):
    matrix = jnp.transpose(snapshots)
    orth, upper = jnp.linalg.qr(matrix)
    signs = jnp.sign(jnp.diagonal(upper))
    upper = upper * signs[:, None]
    orth = orth * signs[None, :]
    total = math.sqrt(matrix.shape[0])
    return (orth * total, upper / total)
```

```python
import math

import jax
import jax.numpy as jnp
from jax import lax
from jax.sharding import PartitionSpec as P

LIMIT = 4096.0


def product(left, right, dims=((1,), (0,))):
    return lax.dot_general(
        left,
        right,
        (dims, ((), ())),
        precision=lax.Precision.HIGHEST,
        preferred_element_type=jnp.float32,
    )


def side_groups(size, side):
    near = [[far * side + step for step in range(side)] for far in range(size // side)]
    across = [[far * side + step for far in range(size // side)] for step in range(side)]
    return near, across


def total(partial):
    near, across = side_groups(lax.axis_size("wide"), 8)
    partial = jnp.sum(lax.all_gather(partial, "narrow"), axis=0)
    partial = jnp.sum(lax.all_gather(partial, "wide", axis_index_groups=near), axis=0)
    return jnp.sum(lax.all_gather(partial, "wide", axis_index_groups=across), axis=0)


def factor(gram):
    lower = jnp.linalg.cholesky(gram)
    eye = jnp.eye(gram.shape[0], dtype=jnp.float32)
    inverse = jax.scipy.linalg.solve_triangular(lower, eye, lower=True)
    spread = jnp.sum(inverse * inverse * jnp.diagonal(gram)[None, :])
    return lower, inverse, spread


def shards(snapshots):
    held, length = snapshots.shape
    groups = lax.axis_size("wide")
    lanes = 128
    pieces = length // groups // lanes
    blocks = snapshots.reshape(held, groups, pieces, lanes).transpose(1, 2, 0, 3)
    blocks = blocks.reshape(groups, pieces * held, lanes)
    blocks = lax.all_to_all(blocks, "wide", split_axis=0, concat_axis=0, tiled=True)
    blocks = blocks.reshape(groups, pieces, held, lanes).transpose(0, 2, 1, 3)
    columns = blocks.reshape(groups * held, pieces * lanes)

    lower, inverse, spread = factor(total(product(columns, columns, ((1,), (1,)))))

    def rough(state):
        step, _, _, spread = state
        return jnp.logical_and(step < 4, jnp.logical_not(spread <= LIMIT))

    def again(state):
        step, inverse, upper, _ = state
        rows = product(inverse, columns)
        lower, more, spread = factor(total(product(rows, rows, ((1,), (1,)))))
        return step + 1, product(more, inverse), product(lower, upper, ((0,), (0,))), spread

    state = (jnp.int32(0), inverse, jnp.transpose(lower), spread)
    _, inverse, upper, _ = lax.while_loop(rough, again, state)
    rows_total = length * lax.axis_size("narrow")
    root = math.sqrt(rows_total)
    return product(columns, inverse * root, ((0,), (1,))), upper / root


def solution(mesh):
    in_specs = (P("wide", "narrow"),)
    out_specs = (P(("narrow", "wide"), None), P())
    return jax.shard_map(shards, mesh=mesh, in_specs=in_specs, out_specs=out_specs, check_vma=False)
```

```python
import math

import jax
import jax.numpy as jnp
from jax import lax
from jax.experimental import pallas as pl
from jax.experimental.pallas import tpu as pltpu
from jax.sharding import PartitionSpec as P

LANES = 128
SUBLANES = 8
PANEL = 16
FLOOR = 1e-6
LIMIT = 4096.0
PASSES = 5


def product(left, right, dims=((1,), (0,))):
    return lax.dot_general(
        left,
        right,
        (dims, ((), ())),
        precision=lax.Precision.HIGHEST,
        preferred_element_type=jnp.float32,
    )


def side_groups(size, side):
    near = [[far * side + step for step in range(side)] for far in range(size // side)]
    across = [[far * side + step for far in range(size // side)] for step in range(side)]
    return near, across


def exchange(pieces, axis, groups=None):
    return lax.all_to_all(
        pieces, axis, split_axis=0, concat_axis=0, axis_index_groups=groups, tiled=True
    )


def total(partial):
    order = partial.shape[0]
    slabs = lax.axis_size("narrow")
    size = lax.axis_size("wide")
    side = math.isqrt(size)
    near, across = side_groups(size, side)
    slab = jnp.sum(exchange(partial.reshape(slabs, order // slabs, order), "narrow"), axis=0)
    slab = jnp.sum(exchange(jnp.broadcast_to(slab, (side, *slab.shape)), "wide", near), axis=0)
    slab = jnp.sum(exchange(jnp.broadcast_to(slab, (side, *slab.shape)), "wide", across), axis=0)
    slab = jnp.broadcast_to(slab, (slabs, *slab.shape))
    return exchange(slab, "narrow").reshape(order, order)


def split(value):
    high = value.astype(jnp.bfloat16)
    rest = value - high.astype(jnp.float32)
    middle = rest.astype(jnp.bfloat16)
    low = (rest - middle.astype(jnp.float32)).astype(jnp.bfloat16)
    return high, middle, low


def replicated(value):
    return jnp.broadcast_to(value, (SUBLANES, LANES))


def stacked(values):
    place = lax.broadcasted_iota(jnp.int32, (SUBLANES, LANES), 0)
    blocks = []
    for first in range(0, len(values), SUBLANES):
        block = values[first]
        for step in range(1, SUBLANES):
            block = jnp.where(place == step, values[first + step], block)
        blocks.append(block)
    return jnp.concatenate(blocks, axis=0)


def factor_kernel(gram_ref, inverse_ref, upper_ref, spread_ref, work):
    order = gram_ref.shape[0]
    gram = gram_ref[...]
    across = lax.broadcasted_iota(jnp.int32, (order, order), 1)
    down = lax.broadcasted_iota(jnp.int32, (order, order), 0)
    diagonal = jnp.where(across == down, gram, 0.0)
    scale = lax.rsqrt(jnp.sum(diagonal, axis=0, keepdims=True))
    work[:, :order] = gram * scale * lax.rsqrt(jnp.sum(diagonal, axis=1, keepdims=True))
    work[:, order:] = jnp.where(across == down, 1.0, 0.0)
    for base in range(0, order, PANEL):
        end = base + PANEL
        panel = work[base:end, base:end]
        entry = {}
        for col in range(PANEL):
            spread_col = jnp.broadcast_to(panel[:, col : col + 1], (PANEL, LANES))
            for row in range(col + 1):
                entry[row, col] = replicated(spread_col[row : row + 1, :])
        left = [replicated(work[base + row : base + row + 1, :order]) for row in range(PANEL)]
        right = [replicated(work[base + row : base + row + 1, order:]) for row in range(PANEL)]
        for pivot in range(PANEL):
            inv = lax.rsqrt(jnp.maximum(entry[pivot, pivot], FLOOR))
            left[pivot] = left[pivot] * inv
            right[pivot] = right[pivot] * inv
            for col in range(pivot + 1, PANEL):
                entry[pivot, col] = entry[pivot, col] * inv
            for col in range(pivot + 1, PANEL):
                ratio = entry[pivot, col]
                for row in range(pivot + 1, col + 1):
                    entry[row, col] = entry[row, col] - entry[pivot, row] * ratio
                left[col] = left[col] - ratio * left[pivot]
                right[col] = right[col] - ratio * right[pivot]
        rows = jnp.concatenate([stacked(left), stacked(right)], axis=1)
        work[base:end, :] = rows
        if end < order:
            high, middle, low = split(rows)
            first = jnp.concatenate([high, high, middle, high, low, middle], axis=0)
            second = jnp.concatenate([high, middle, high, low, high, middle], axis=0)
            update = lax.dot_general(
                first[:, :order],
                second,
                (((0,), (0,)), ((), ())),
                preferred_element_type=jnp.float32,
            )
            work[end:, :] -= update[end:, :]
    inverse = jnp.where(across <= down, work[:, order:], 0.0)
    spread_ref[...] = jnp.full(spread_ref.shape, jnp.sum(inverse * inverse))
    inverse_ref[...] = inverse * scale
    upper_ref[...] = jnp.where(across >= down, work[:, :order], 0.0) * (1.0 / scale)


def factor(gram):
    order = gram.shape[0]
    square = jax.ShapeDtypeStruct((order, order), jnp.float32)
    whole = pl.BlockSpec(memory_space=pltpu.VMEM)
    inverse, upper, spread = pl.pallas_call(
        factor_kernel,
        out_shape=[square, square, jax.ShapeDtypeStruct((SUBLANES, LANES), jnp.float32)],
        in_specs=[whole],
        out_specs=[whole] * 3,
        scratch_shapes=[pltpu.VMEM((order, 2 * order), jnp.float32)],
        name="factor",
    )(gram)
    return inverse, upper, spread[0, 0]


def shards(snapshots):
    held, length = snapshots.shape
    groups = lax.axis_size("wide")
    tiles = length // LANES
    blocks = snapshots.reshape(held, tiles, LANES).transpose(1, 0, 2)
    blocks = exchange(blocks, "wide").reshape(groups, tiles // groups, held, LANES)
    columns = blocks.transpose(0, 2, 1, 3).reshape(groups * held, length // groups)

    inverse, upper, spread = factor(total(product(columns, columns, ((1,), (1,)))))

    def rough(state):
        step, _, _, spread = state
        return jnp.logical_and(step < PASSES, jnp.logical_not(spread <= LIMIT))

    def again(state):
        step, inverse, upper, _ = state
        rows = product(inverse, columns)
        more, next_upper, spread = factor(total(product(rows, rows, ((1,), (1,)))))
        return step + 1, product(more, inverse), product(next_upper, upper), spread

    _, inverse, upper, _ = lax.while_loop(rough, again, (jnp.int32(1), inverse, upper, spread))
    root = math.sqrt(length * lax.axis_size("narrow"))
    return product(columns, inverse * root, ((0,), (1,))), upper / root


def solution(mesh):
    in_specs = (P("wide", "narrow"),)
    out_specs = (P(("narrow", "wide"), None), P())
    return jax.shard_map(shards, mesh=mesh, in_specs=in_specs, out_specs=out_specs, check_vma=False)
```

```python
import functools
import math

import jax
import jax.numpy as jnp
from jax import lax
from jax.experimental import pallas as pl
from jax.experimental.pallas import tpu as pltpu
from jax.sharding import PartitionSpec as P

LANES = 128
SUBLANES = 8
PANEL = 16
FLOOR = 1e-6
LIMIT = 4096.0
PASSES = 5


def product(left, right, dims=((1,), (0,))):
    return lax.dot_general(
        left,
        right,
        (dims, ((), ())),
        precision=lax.Precision.HIGHEST,
        preferred_element_type=jnp.float32,
    )


def exchange(pieces, axis, groups=None):
    return lax.all_to_all(
        pieces, axis, split_axis=0, concat_axis=0, axis_index_groups=groups, tiled=True
    )


def members(axis, stride, count):
    size = lax.axis_size(axis)
    return [
        [first + step * stride for step in range(count)]
        for block in range(0, size, stride * count)
        for first in range(block, block + stride)
    ]


def added(part, axis, stride, count):
    pieces = jnp.broadcast_to(part, (count, *part.shape))
    return jnp.sum(exchange(pieces, axis, members(axis, stride, count)), axis=0)


def paired(part):
    return lax.all_gather(part, "narrow", axis_index_groups=members("narrow", 1, 2))


def total(packed):
    half = packed.shape[0] // 2
    both = jnp.sum(paired(packed), axis=0)
    part = lax.dynamic_slice_in_dim(both, lax.axis_index("narrow") % 2 * half, half, axis=0)
    side = math.isqrt(lax.axis_size("wide"))
    part = added(part, "narrow", 2, lax.axis_size("narrow") // 2)
    part = added(part, "wide", 1, side)
    part = added(part, "wide", side, lax.axis_size("wide") // side)
    return paired(part).reshape(packed.shape)


def gram_kernel(columns_ref, packed_ref):
    columns = columns_ref[...]
    gram = product(columns, columns, ((1,), (1,)))
    half = gram.shape[0] // 2
    across = lax.broadcasted_iota(jnp.int32, (half, 2 * half), 1)
    down = lax.broadcasted_iota(jnp.int32, (half, 2 * half), 0)
    bottom = gram[half:, :]
    packed_ref[:half, :] = jnp.where(across < down, pltpu.roll(bottom, half, 1), gram[:half, :])
    corner = jnp.sum(jnp.where(across == down + half, bottom, 0.0), axis=0, keepdims=True)
    rest = packed_ref.shape[0] - half
    packed_ref[half:, :] = jnp.broadcast_to(corner, (rest, 2 * half))


def gram(columns):
    order = columns.shape[0]
    rows = order // 2 + 2 * SUBLANES
    return pl.pallas_call(
        gram_kernel,
        out_shape=jax.ShapeDtypeStruct((rows, order), jnp.float32),
        in_specs=[pl.BlockSpec(memory_space=pltpu.VMEM)],
        out_specs=pl.BlockSpec(memory_space=pltpu.VMEM),
        name="gram",
    )(columns)


def split(value):
    high = value.astype(jnp.bfloat16)
    rest = value - high.astype(jnp.float32)
    middle = rest.astype(jnp.bfloat16)
    low = (rest - middle.astype(jnp.float32)).astype(jnp.bfloat16)
    return high, middle, low


def replicated(value):
    return jnp.broadcast_to(value, (SUBLANES, LANES))


def stacked(values):
    place = lax.broadcasted_iota(jnp.int32, (SUBLANES, LANES), 0)
    blocks = []
    for first in range(0, len(values), SUBLANES):
        block = values[first]
        for step in range(1, SUBLANES):
            block = jnp.where(place == step, values[first + step], block)
        blocks.append(block)
    return jnp.concatenate(blocks, axis=0)


def factor_kernel(root, packed_ref, inverse_ref, upper_ref, spread_ref, work):
    order = packed_ref.shape[1]
    half = order // 2
    across = lax.broadcasted_iota(jnp.int32, (order, order), 1)
    down = lax.broadcasted_iota(jnp.int32, (order, order), 0)
    top = packed_ref[:half, :]
    flipped = pltpu.roll(jnp.transpose(jnp.concatenate([top, top], axis=0))[:half, :], half, 1)
    bottom = jnp.where((across == down + half)[:half, :], packed_ref[half : half + 1, :], flipped)
    gram = jnp.concatenate([top, bottom], axis=0)
    diagonal = jnp.where(across == down, gram, 0.0)
    scale = lax.rsqrt(jnp.sum(diagonal, axis=0, keepdims=True))
    work[:, :order] = gram * scale * lax.rsqrt(jnp.sum(diagonal, axis=1, keepdims=True))
    work[:, order:] = jnp.where(across == down, 1.0, 0.0)
    for base in range(0, order, PANEL):
        end = base + PANEL
        panel = work[base:end, base:end]
        entry = {}
        for col in range(PANEL):
            spread_col = jnp.broadcast_to(panel[:, col : col + 1], (PANEL, LANES))
            for row in range(col + 1):
                entry[row, col] = replicated(spread_col[row : row + 1, :])
        left = [replicated(work[base + row : base + row + 1, :order]) for row in range(PANEL)]
        right = [replicated(work[base + row : base + row + 1, order:]) for row in range(PANEL)]
        for pivot in range(PANEL):
            inv = lax.rsqrt(jnp.maximum(entry[pivot, pivot], FLOOR))
            left[pivot] = left[pivot] * inv
            right[pivot] = right[pivot] * inv
            for col in range(pivot + 1, PANEL):
                entry[pivot, col] = entry[pivot, col] * inv
            for col in range(pivot + 1, PANEL):
                ratio = entry[pivot, col]
                for row in range(pivot + 1, col + 1):
                    entry[row, col] = entry[row, col] - entry[pivot, row] * ratio
                left[col] = left[col] - ratio * left[pivot]
                right[col] = right[col] - ratio * right[pivot]
        rows = jnp.concatenate([stacked(left), stacked(right)], axis=1)
        work[base:end, :] = rows
        if end < order:
            high, middle, low = split(rows)
            first = jnp.concatenate([high, high, middle, high, low, middle], axis=0)
            second = jnp.concatenate([high, middle, high, low, high, middle], axis=0)
            update = lax.dot_general(
                first[:, :order],
                second,
                (((0,), (0,)), ((), ())),
                preferred_element_type=jnp.float32,
            )
            work[end:, :] -= update[end:, :]
    inverse = jnp.where(across <= down, work[:, order:], 0.0)
    spread_ref[...] = jnp.sum(inverse * inverse, keepdims=True)
    inverse_ref[...] = inverse * (scale * root)
    upper_ref[...] = jnp.where(across >= down, work[:, :order], 0.0) * (1.0 / (scale * root))


def factor(packed, root):
    order = packed.shape[1]
    square = jax.ShapeDtypeStruct((order, order), jnp.float32)
    whole = pl.BlockSpec(memory_space=pltpu.VMEM)
    inverse, upper, spread = pl.pallas_call(
        functools.partial(factor_kernel, root),
        out_shape=[square, square, jax.ShapeDtypeStruct((1, 1), jnp.float32)],
        in_specs=[whole],
        out_specs=[whole] * 3,
        scratch_shapes=[pltpu.VMEM((order, 2 * order), jnp.float32)],
        name="factor",
    )(packed)
    return inverse, upper, spread.reshape(())


def apply_kernel(columns_ref, inverse_ref, rows_ref):
    rows_ref[...] = product(columns_ref[...], inverse_ref[...], ((0,), (1,)))


def apply(columns, inverse):
    order, length = columns.shape
    step = math.gcd(length, 2 * LANES)
    return pl.pallas_call(
        apply_kernel,
        out_shape=jax.ShapeDtypeStruct((length, order), jnp.float32),
        grid=(length // step,),
        in_specs=[
            pl.BlockSpec((order, step), lambda i: (0, i)),
            pl.BlockSpec((order, order), lambda i: (0, 0)),
        ],
        out_specs=pl.BlockSpec((step, order), lambda i: (i, 0)),
        name="apply",
    )(columns, inverse)


def shards(snapshots):
    held, length = snapshots.shape
    groups = lax.axis_size("wide")
    tiles = length // LANES
    blocks = snapshots.reshape(held, tiles, LANES).transpose(1, 0, 2)
    blocks = exchange(blocks, "wide").reshape(groups, tiles // groups, held, LANES)
    columns = blocks.transpose(0, 2, 1, 3).reshape(groups * held, length // groups)

    root = math.sqrt(length * lax.axis_size("narrow"))

    inverse, upper, spread = factor(total(gram(columns)), root)

    def rough(state):
        step, _, _, spread = state
        return jnp.logical_and(step < PASSES, jnp.logical_not(spread <= LIMIT))

    def again(state):
        step, inverse, upper, _ = state
        more, next_upper, spread = factor(total(gram(product(inverse, columns))), root)
        return step + 1, product(more, inverse), product(next_upper, upper), spread

    _, inverse, upper, _ = lax.while_loop(rough, again, (jnp.int32(1), inverse, upper, spread))
    return apply(columns, inverse), upper


def solution(mesh):
    in_specs = (P("wide", "narrow"),)
    out_specs = (P(("narrow", "wide"), None), P())
    return jax.shard_map(shards, mesh=mesh, in_specs=in_specs, out_specs=out_specs, check_vma=False)
```

```python
import functools
import math

import jax
import jax.numpy as jnp
import numpy as np
from jax import lax
from jax.experimental import pallas as pl
from jax.experimental.pallas import tpu as pltpu
from jax.sharding import PartitionSpec as P

LANES = 128
SUBLANES = 8
PANEL = 16
FLOOR = 1e-6
LIMIT = 4096.0
PASSES = 5


def product(left, right, dims=((1,), (0,))):
    return lax.dot_general(
        left,
        right,
        (dims, ((), ())),
        precision=lax.Precision.HIGHEST,
        preferred_element_type=jnp.float32,
    )


def exchange(pieces, axis, groups=None):
    return lax.all_to_all(
        pieces, axis, split_axis=0, concat_axis=0, axis_index_groups=groups, tiled=True
    )


EVERY = ("wide", "narrow")


def added(part, groups):
    pieces = jnp.broadcast_to(part, (len(groups[0]), *part.shape))
    return jnp.sum(exchange(pieces, EVERY, groups), axis=0)


def paired(part, groups):
    return lax.all_gather(part, EVERY, axis_index_groups=groups)


def total(packed):
    wide, narrow = lax.axis_size("wide"), lax.axis_size("narrow")
    side = math.isqrt(wide)
    places = np.arange(wide * narrow).reshape(wide // side, side, narrow // 2, 2)
    pairs = places.reshape(-1, 2).tolist()
    spread = places.transpose(0, 1, 3, 2).reshape(-1, narrow // 2).tolist()
    near = places.transpose(3, 2, 0, 1)
    far = places.transpose(3, 2, 1, 0)
    first = [near[0].reshape(-1, side), far[1].reshape(-1, wide // side)]
    second = [far[0].reshape(-1, wide // side), near[1].reshape(-1, side)]
    half = packed.shape[0] // 2
    both = jnp.sum(paired(packed, pairs), axis=0)
    part = lax.dynamic_slice_in_dim(both, lax.axis_index("narrow") % 2 * half, half, axis=0)
    part = added(part, spread)
    part = added(part, np.concatenate(first).tolist())
    part = added(part, np.concatenate(second).tolist())
    return paired(part, pairs).reshape(packed.shape)


def gram(values, dim):
    square = product(values, values, ((dim,), (dim,)))
    half = square.shape[0] // 2
    across = lax.broadcasted_iota(jnp.int32, (half, 2 * half), 1)
    down = lax.broadcasted_iota(jnp.int32, (half, 2 * half), 0)
    bottom = square[half:, :]
    rows = jnp.where(across < down, jnp.roll(bottom, half, axis=1), square[:half, :])
    corner = jnp.sum(jnp.where(across == down + half, bottom, 0.0), axis=0, keepdims=True)
    return jnp.concatenate([rows, jnp.broadcast_to(corner, (2 * SUBLANES, 2 * half))], axis=0)


def split(value):
    high = value.astype(jnp.bfloat16)
    rest = value - high.astype(jnp.float32)
    middle = rest.astype(jnp.bfloat16)
    low = (rest - middle.astype(jnp.float32)).astype(jnp.bfloat16)
    return high, middle, low


def replicated(value):
    return jnp.broadcast_to(value, (SUBLANES, LANES))


def stacked(values):
    place = lax.broadcasted_iota(jnp.int32, (SUBLANES, LANES), 0)
    blocks = []
    for first in range(0, len(values), SUBLANES):
        block = values[first]
        for step in range(1, SUBLANES):
            block = jnp.where(place == step, values[first + step], block)
        blocks.append(block)
    return jnp.concatenate(blocks, axis=0)


def factor_kernel(root, packed_ref, inverse_ref, upper_ref, status_ref, work):
    order = packed_ref.shape[1]
    half = order // 2
    across = lax.broadcasted_iota(jnp.int32, (order, order), 1)
    down = lax.broadcasted_iota(jnp.int32, (order, order), 0)
    top = packed_ref[:half, :]
    flipped = pltpu.roll(jnp.transpose(jnp.concatenate([top, top], axis=0))[:half, :], half, 1)
    bottom = jnp.where((across == down + half)[:half, :], packed_ref[half : half + 1, :], flipped)
    gram = jnp.concatenate([top, bottom], axis=0)
    diagonal = jnp.where(across == down, gram, 0.0)
    scale = lax.rsqrt(jnp.sum(diagonal, axis=0, keepdims=True))
    work[:, :order] = gram * scale * lax.rsqrt(jnp.sum(diagonal, axis=1, keepdims=True))
    work[:, order:] = jnp.where(across == down, 1.0, 0.0)
    for base in range(0, order, PANEL):
        end = base + PANEL
        panel = work[base:end, base:end]
        entry = {}
        for col in range(PANEL):
            spread_col = jnp.broadcast_to(panel[:, col : col + 1], (PANEL, LANES))
            for row in range(col + 1):
                entry[row, col] = replicated(spread_col[row : row + 1, :])
        left = [replicated(work[base + row : base + row + 1, :order]) for row in range(PANEL)]
        right = [replicated(work[base + row : base + row + 1, order:]) for row in range(PANEL)]
        for pivot in range(PANEL):
            inv = lax.rsqrt(jnp.maximum(entry[pivot, pivot], FLOOR))
            left[pivot] = left[pivot] * inv
            right[pivot] = right[pivot] * inv
            for col in range(pivot + 1, PANEL):
                entry[pivot, col] = entry[pivot, col] * inv
            for col in range(pivot + 1, PANEL):
                ratio = entry[pivot, col]
                for row in range(pivot + 1, col + 1):
                    entry[row, col] = entry[row, col] - entry[pivot, row] * ratio
                left[col] = left[col] - ratio * left[pivot]
                right[col] = right[col] - ratio * right[pivot]
        rows = jnp.concatenate([stacked(left), stacked(right)], axis=1)
        work[base:end, :] = rows
        if end < order:
            high, middle, low = split(rows)
            first = jnp.concatenate([high, high, middle, high, low, middle], axis=0)
            second = jnp.concatenate([high, middle, high, low, high, middle], axis=0)
            update = lax.dot_general(
                first[:, :order],
                second,
                (((0,), (0,)), ((), ())),
                preferred_element_type=jnp.float32,
            )
            work[end:, :] -= update[end:, :]
    inverse = jnp.where(across <= down, work[:, order:], 0.0)
    place = lax.broadcasted_iota(jnp.int32, status_ref.shape, 1)
    status_ref[...] = jnp.where(place == 0, jnp.sum(inverse * inverse, keepdims=True), 0.0)
    inverse_ref[...] = inverse * (scale * root)
    upper_ref[...] = jnp.where(across >= down, work[:, :order], 0.0) * (1.0 / (scale * root))


def factor(packed, root):
    order = packed.shape[1]
    shape = jax.ShapeDtypeStruct((order, order), jnp.float32)
    whole = pl.BlockSpec(memory_space=pltpu.VMEM)
    return pl.pallas_call(
        functools.partial(factor_kernel, root),
        out_shape=[shape, shape, jax.ShapeDtypeStruct((1, 2), jnp.float32)],
        in_specs=[whole],
        out_specs=[whole] * 3,
        scratch_shapes=[pltpu.VMEM((order, 2 * order), jnp.float32)],
        name="factor",
    )(packed)


def apply_kernel(tiles_ref, inverse_ref, rows_ref, buffer, done):
    blocks = done.shape[0]
    order = inverse_ref.shape[0]
    copies = []
    for block in range(blocks):
        part = pl.ds(block * LANES, LANES)
        values = tiles_ref[pl.ds(block, order, stride=blocks), :]
        buffer[part, :] = product(values, inverse_ref[...], ((0,), (1,)))
        copies.append(
            pltpu.make_async_copy(buffer.at[part, :], rows_ref.at[part, :], done.at[block])
        )
        copies[-1].start()
    for copy in copies:
        copy.wait()


def apply(tiles, inverse):
    order = inverse.shape[0]
    blocks = tiles.shape[0] // order
    whole = pl.BlockSpec(memory_space=pltpu.VMEM)
    return pl.pallas_call(
        apply_kernel,
        out_shape=jax.ShapeDtypeStruct((blocks * LANES, order), jnp.float32),
        in_specs=[whole, whole],
        out_specs=pl.BlockSpec(memory_space=pl.ANY),
        scratch_shapes=[
            pltpu.VMEM((blocks * LANES, order), jnp.float32),
            pltpu.SemaphoreType.DMA((blocks,)),
        ],
        name="apply",
    )(tiles, inverse)


def shards(snapshots):
    held, length = snapshots.shape
    groups = lax.axis_size("wide")
    tiles = length // LANES
    blocks = snapshots.reshape(held, tiles, LANES).transpose(1, 0, 2)
    blocks = exchange(blocks, "wide").reshape(groups, tiles // groups, held, LANES)
    tiles = blocks.transpose(0, 2, 1, 3).reshape(-1, LANES)
    columns = tiles.reshape(groups * held, length // groups)

    root = math.sqrt(length * lax.axis_size("narrow"))

    inverse, upper, status = factor(total(gram(columns, 1)), root)

    def rough(state):
        status = state[2]
        return jnp.logical_and(status[0, 1] < PASSES - 1, jnp.logical_not(status[0, 0] <= LIMIT))

    def again(state):
        inverse, upper, status = state
        more, next_upper, fresh = factor(total(gram(apply(tiles, inverse), 0)), root)
        status = jnp.concatenate([fresh[:, :1], status[:, 1:] + 1.0], axis=1)
        return product(more, inverse), product(next_upper, upper), status

    inverse, upper, _ = lax.while_loop(rough, again, (inverse, upper, status))
    return apply(tiles, inverse), upper


def solution(mesh):
    in_specs = (P("wide", "narrow"),)
    out_specs = (P(("narrow", "wide"), None), P())
    return jax.shard_map(shards, mesh=mesh, in_specs=in_specs, out_specs=out_specs, check_vma=False)
```

```python
import functools
import math

import jax
import jax.numpy as jnp
import numpy as np
from jax import lax
from jax.experimental import pallas as pl
from jax.experimental.pallas import tpu as pltpu
from jax.sharding import PartitionSpec as P

LANES = 128
SUBLANES = 8
PANEL = 16
FLOOR = 1e-6
LIMIT = 4096.0
CAP = 1e9
GAIN = 64.0
COPIES = 4


def product(left, right, dims=((1,), (0,))):
    return lax.dot_general(
        left,
        right,
        (dims, ((), ())),
        precision=lax.Precision.HIGHEST,
        preferred_element_type=jnp.float32,
    )


def exchange(pieces, axis, groups=None):
    return lax.all_to_all(
        pieces, axis, split_axis=0, concat_axis=0, axis_index_groups=groups, tiled=True
    )


EVERY = ("wide", "narrow")


def added(part, groups):
    pieces = jnp.broadcast_to(part, (len(groups[0]), *part.shape))
    return jnp.sum(exchange(pieces, EVERY, groups), axis=0)


def paired(part, groups):
    return lax.all_gather(part, EVERY, axis_index_groups=groups)


def total(packed):
    wide, narrow = lax.axis_size("wide"), lax.axis_size("narrow")
    side = math.isqrt(wide)
    places = np.arange(wide * narrow).reshape(side // 2, 2, side // 2, 2, narrow // 2, 2)
    pairs = places.reshape(-1, 2).tolist()
    even, odd = places[..., 0], places[..., 1]
    first = [even.transpose(0, 1, 3, 4, 2), odd.transpose(1, 2, 3, 4, 0)]
    second = [even.transpose(2, 4, 3, 0, 1), odd.transpose(0, 4, 1, 2, 3)]
    first = np.concatenate([part.reshape(-1, narrow // 2 * (side // 2)) for part in first])
    second = np.concatenate([part.reshape(-1, 2 * side) for part in second])
    half = packed.shape[0] // 2
    both = jnp.sum(paired(packed, pairs), axis=0)
    part = lax.dynamic_slice_in_dim(both, lax.axis_index("narrow") % 2 * half, half, axis=0)
    part = added(part, first.tolist())
    part = added(part, second.tolist())
    return paired(part, pairs).reshape(packed.shape)


def gram(values, dim):
    square = product(values, values, ((dim,), (dim,)))
    half = square.shape[0] // 2
    across = lax.broadcasted_iota(jnp.int32, (half, 2 * half), 1)
    down = lax.broadcasted_iota(jnp.int32, (half, 2 * half), 0)
    bottom = square[half:, :]
    rows = jnp.where(across < down, jnp.roll(bottom, half, axis=1), square[:half, :])
    corner = jnp.sum(jnp.where(across == down + half, bottom, 0.0), axis=0, keepdims=True)
    return jnp.concatenate([rows, jnp.broadcast_to(corner, (2 * SUBLANES, 2 * half))], axis=0)


def split(value):
    high = value.astype(jnp.bfloat16)
    rest = value - high.astype(jnp.float32)
    middle = rest.astype(jnp.bfloat16)
    low = (rest - middle.astype(jnp.float32)).astype(jnp.bfloat16)
    return high, middle, low


def replicated(value):
    return jnp.broadcast_to(value, (SUBLANES, LANES))


def stacked(values):
    place = lax.broadcasted_iota(jnp.int32, (SUBLANES, LANES), 0)
    blocks = []
    for first in range(0, len(values), SUBLANES):
        block = values[first]
        for step in range(1, SUBLANES):
            block = jnp.where(place == step, values[first + step], block)
        blocks.append(block)
    return jnp.concatenate(blocks, axis=0)


def factor_kernel(root, packed_ref, inverse_ref, upper_ref, spread_ref, work):
    order = packed_ref.shape[1]
    half = order // 2
    across = lax.broadcasted_iota(jnp.int32, (order, order), 1)
    down = lax.broadcasted_iota(jnp.int32, (order, order), 0)
    top = packed_ref[:half, :]
    flipped = pltpu.roll(jnp.transpose(jnp.concatenate([top, top], axis=0))[:half, :], half, 1)
    bottom = jnp.where((across == down + half)[:half, :], packed_ref[half : half + 1, :], flipped)
    gram = jnp.concatenate([top, bottom], axis=0)
    diagonal = jnp.where(across == down, gram, 0.0)
    scale = lax.rsqrt(jnp.sum(diagonal, axis=0, keepdims=True))
    work[:, :order] = gram * scale * lax.rsqrt(jnp.sum(diagonal, axis=1, keepdims=True))
    work[:, order:] = jnp.where(across == down, 1.0, 0.0)
    for base in range(0, order, PANEL):
        end = base + PANEL
        panel = work[base:end, base:end]
        entry = {}
        for col in range(PANEL):
            spread_col = jnp.broadcast_to(panel[:, col : col + 1], (PANEL, LANES))
            for row in range(col + 1):
                entry[row, col] = replicated(spread_col[row : row + 1, :])
        left = [replicated(work[base + row : base + row + 1, :order]) for row in range(PANEL)]
        right = [replicated(work[base + row : base + row + 1, order:]) for row in range(PANEL)]
        for pivot in range(PANEL):
            inv = lax.rsqrt(jnp.maximum(entry[pivot, pivot], FLOOR))
            left[pivot] = left[pivot] * inv
            right[pivot] = right[pivot] * inv
            for col in range(pivot + 1, PANEL):
                entry[pivot, col] = entry[pivot, col] * inv
            for col in range(pivot + 1, PANEL):
                ratio = entry[pivot, col]
                for row in range(pivot + 1, col + 1):
                    entry[row, col] = entry[row, col] - entry[pivot, row] * ratio
                left[col] = left[col] - ratio * left[pivot]
                right[col] = right[col] - ratio * right[pivot]
        rows = jnp.concatenate([stacked(left), stacked(right)], axis=1)
        work[base:end, :] = rows
        if end < order:
            high, middle, low = split(rows)
            first = jnp.concatenate([high, high, middle, high, low, middle], axis=0)
            second = jnp.concatenate([high, middle, high, low, high, middle], axis=0)
            update = lax.dot_general(
                first[:, :order],
                second,
                (((0,), (0,)), ((), ())),
                preferred_element_type=jnp.float32,
            )
            work[end:, :] -= update[end:, :]
    inverse = jnp.where(across <= down, work[:, order:], 0.0)
    spread_ref[...] = jnp.minimum(jnp.sum(inverse * inverse, keepdims=True), CAP)
    inverse_ref[...] = inverse * (scale * root)
    upper_ref[...] = jnp.where(across >= down, work[:, :order], 0.0) * (1.0 / (scale * root))


def factor(packed, root):
    order = packed.shape[1]
    shape = jax.ShapeDtypeStruct((order, order), jnp.float32)
    whole = pl.BlockSpec(memory_space=pltpu.VMEM)
    inverse, upper, spread = pl.pallas_call(
        functools.partial(factor_kernel, root),
        out_shape=[shape, shape, jax.ShapeDtypeStruct((1, 1), jnp.float32)],
        in_specs=[whole],
        out_specs=[whole] * 3,
        scratch_shapes=[pltpu.VMEM((order, 2 * order), jnp.float32)],
        name="factor",
    )(packed)
    return inverse, upper, spread.reshape(())


def apply_kernel(tiles_ref, inverse_ref, rows_ref, buffer, done):
    order = inverse_ref.shape[0]
    blocks = tiles_ref.shape[0] // order
    group = blocks // done.shape[0]
    copies = []
    for block in range(blocks):
        values = tiles_ref[pl.ds(block, order, stride=blocks), :]
        place = pl.ds(block * LANES, LANES)
        buffer[place, :] = product(values, inverse_ref[...], ((0,), (1,)))
        if block % group == group - 1:
            part = pl.ds((block + 1 - group) * LANES, group * LANES)
            copies.append(
                pltpu.make_async_copy(
                    buffer.at[part, :], rows_ref.at[part, :], done.at[block // group]
                )
            )
            copies[-1].start()
    for copy in copies:
        copy.wait()


def apply(tiles, inverse):
    order = inverse.shape[0]
    blocks = tiles.shape[0] // order
    whole = pl.BlockSpec(memory_space=pltpu.VMEM)
    return pl.pallas_call(
        apply_kernel,
        out_shape=jax.ShapeDtypeStruct((blocks * LANES, order), jnp.float32),
        in_specs=[whole, whole],
        out_specs=pl.BlockSpec(memory_space=pl.ANY),
        scratch_shapes=[
            pltpu.VMEM((blocks * LANES, order), jnp.float32),
            pltpu.SemaphoreType.DMA((math.gcd(blocks, COPIES),)),
        ],
        name="apply",
    )(tiles, inverse)


def shards(snapshots):
    held, length = snapshots.shape
    groups = lax.axis_size("wide")
    tiles = length // LANES
    blocks = snapshots.reshape(held, tiles, LANES).transpose(1, 0, 2)
    blocks = exchange(blocks, "wide").reshape(groups, tiles // groups, held, LANES)
    tiles = blocks.transpose(0, 2, 1, 3).reshape(-1, LANES)
    columns = tiles.reshape(groups * held, length // groups)

    root = math.sqrt(length * lax.axis_size("narrow"))

    inverse, upper, spread = factor(total(gram(columns, 1)), root)

    def rough(state):
        return state[2] > LIMIT

    def again(state):
        inverse, upper, spread = state
        more, next_upper, fresh = factor(total(gram(apply(tiles, inverse), 0)), root)
        fresh = jnp.minimum(fresh, spread / GAIN)
        return product(more, inverse), product(next_upper, upper), fresh

    inverse, upper, _ = lax.while_loop(rough, again, (inverse, upper, spread))
    return apply(tiles, inverse), upper


def solution(mesh):
    in_specs = (P("wide", "narrow"),)
    out_specs = (P(("narrow", "wide"), None), P())
    return jax.shard_map(shards, mesh=mesh, in_specs=in_specs, out_specs=out_specs, check_vma=False)
```

```python
import functools
import math

import jax
import jax.numpy as jnp
import numpy as np
from jax import lax
from jax.experimental import pallas as pl
from jax.experimental.pallas import tpu as pltpu
from jax.sharding import PartitionSpec as P

LANES = 128
SUBLANES = 8
PANEL = 16
FLOOR = 1e-6
LIMIT = 4096.0
CAP = 1e9
GAIN = 64.0


def product(left, right, dims=((1,), (0,))):
    return lax.dot_general(
        left,
        right,
        (dims, ((), ())),
        precision=lax.Precision.HIGHEST,
        preferred_element_type=jnp.float32,
    )


def exchange(pieces, axis, groups=None):
    return lax.all_to_all(
        pieces, axis, split_axis=0, concat_axis=0, axis_index_groups=groups, tiled=True
    )


EVERY = ("wide", "narrow")


def added(part, groups):
    pieces = jnp.broadcast_to(part, (len(groups[0]), *part.shape))
    return jnp.sum(exchange(pieces, EVERY, groups), axis=0)


def paired(part, groups):
    return lax.all_gather(part, EVERY, axis_index_groups=groups)


def total(packed):
    wide, narrow = lax.axis_size("wide"), lax.axis_size("narrow")
    side = math.isqrt(wide)
    places = np.arange(wide * narrow).reshape(side // 2, 2, side // 2, 2, narrow // 2, 2)
    pairs = places.reshape(-1, 2).tolist()
    even, odd = places[..., 0], places[..., 1]
    first = [even.transpose(0, 1, 3, 4, 2), odd.transpose(1, 2, 3, 4, 0)]
    second = [even.transpose(2, 4, 3, 0, 1), odd.transpose(0, 4, 1, 2, 3)]
    first = np.concatenate([part.reshape(-1, narrow // 2 * (side // 2)) for part in first])
    second = np.concatenate([part.reshape(-1, 2 * side) for part in second])
    half = packed.shape[0] // 2
    both = jnp.sum(paired(packed, pairs), axis=0)
    part = lax.dynamic_slice_in_dim(both, lax.axis_index("narrow") % 2 * half, half, axis=0)
    part = added(part, first.tolist())
    part = added(part, second.tolist())
    return paired(part, pairs).reshape(packed.shape)


def gram(values, dim):
    square = product(values, values, ((dim,), (dim,)))
    half = square.shape[0] // 2
    across = lax.broadcasted_iota(jnp.int32, (half, 2 * half), 1)
    down = lax.broadcasted_iota(jnp.int32, (half, 2 * half), 0)
    bottom = square[half:, :]
    rows = jnp.where(across < down, jnp.roll(bottom, half, axis=1), square[:half, :])
    corner = jnp.sum(jnp.where(across == down + half, bottom, 0.0), axis=0, keepdims=True)
    return jnp.concatenate([rows, jnp.broadcast_to(corner, (2 * SUBLANES, 2 * half))], axis=0)


def split(value):
    high = value.astype(jnp.bfloat16)
    rest = value - high.astype(jnp.float32)
    middle = rest.astype(jnp.bfloat16)
    low = (rest - middle.astype(jnp.float32)).astype(jnp.bfloat16)
    return high, middle, low


def bf16_product(left, right):
    return jnp.dot(left, right, preferred_element_type=jnp.float32)


def replicated(value):
    return jnp.broadcast_to(value, (SUBLANES, LANES))


def stacked(values):
    place = lax.broadcasted_iota(jnp.int32, (SUBLANES, LANES), 0)
    blocks = []
    for first in range(0, len(values), SUBLANES):
        block = values[first]
        for step in range(1, SUBLANES):
            block = jnp.where(place == step, values[first + step], block)
        blocks.append(block)
    return jnp.concatenate(blocks, axis=0)


def factor_kernel(root, packed_ref, inverse_ref, upper_ref, spread_ref, work):
    order = packed_ref.shape[1]
    half = order // 2
    across = lax.broadcasted_iota(jnp.int32, (order, order), 1)
    down = lax.broadcasted_iota(jnp.int32, (order, order), 0)
    top = packed_ref[:half, :]
    flipped = pltpu.roll(jnp.transpose(jnp.concatenate([top, top], axis=0))[:half, :], half, 1)
    bottom = jnp.where((across == down + half)[:half, :], packed_ref[half : half + 1, :], flipped)
    gram = jnp.concatenate([top, bottom], axis=0)
    diagonal = jnp.where(across == down, gram, 0.0)
    scale = lax.rsqrt(jnp.sum(diagonal, axis=0, keepdims=True))
    work[:, :order] = gram * scale * lax.rsqrt(jnp.sum(diagonal, axis=1, keepdims=True))
    work[:, order:] = jnp.where(across == down, 1.0, 0.0)
    for base in range(0, order, PANEL):
        end = base + PANEL
        panel = work[base:end, base:end]
        entry = {}
        for col in range(PANEL):
            spread_col = jnp.broadcast_to(panel[:, col : col + 1], (PANEL, LANES))
            for row in range(col + 1):
                entry[row, col] = replicated(spread_col[row : row + 1, :])
        left = [replicated(work[base + row : base + row + 1, :order]) for row in range(PANEL)]
        right = [replicated(work[base + row : base + row + 1, order:]) for row in range(PANEL)]
        for pivot in range(PANEL):
            inv = lax.rsqrt(jnp.maximum(entry[pivot, pivot], FLOOR))
            left[pivot] = left[pivot] * inv
            right[pivot] = right[pivot] * inv
            for col in range(pivot + 1, PANEL):
                entry[pivot, col] = entry[pivot, col] * inv
            for col in range(pivot + 1, PANEL):
                ratio = entry[pivot, col]
                for row in range(pivot + 1, col + 1):
                    entry[row, col] = entry[row, col] - entry[pivot, row] * ratio
                left[col] = left[col] - ratio * left[pivot]
                right[col] = right[col] - ratio * right[pivot]
        rows = jnp.concatenate([stacked(left), stacked(right)], axis=1)
        work[base:end, :] = rows
        if end < order:
            high, middle, low = split(rows)
            first = jnp.concatenate([high, high, middle, high, low, middle], axis=0)
            second = jnp.concatenate([high, middle, high, low, high, middle], axis=0)
            update = lax.dot_general(
                first[:, :order],
                second,
                (((0,), (0,)), ((), ())),
                preferred_element_type=jnp.float32,
            )
            work[end:, :] -= update[end:, :]
    inverse = jnp.where(across <= down, work[:, order:], 0.0)
    spread_ref[...] = jnp.minimum(jnp.sum(inverse * inverse, keepdims=True), CAP)
    inverse_ref[...] = inverse * (scale * root)
    upper_ref[...] = jnp.where(across >= down, work[:, :order], 0.0) * (1.0 / (scale * root))


def factor(packed, root):
    order = packed.shape[1]
    shape = jax.ShapeDtypeStruct((order, order), jnp.float32)
    whole = pl.BlockSpec(memory_space=pltpu.VMEM)
    inverse, upper, spread = pl.pallas_call(
        functools.partial(factor_kernel, root),
        out_shape=[shape, shape, jax.ShapeDtypeStruct((1, 1), jnp.float32)],
        in_specs=[whole],
        out_specs=[whole] * 3,
        scratch_shapes=[pltpu.VMEM((order, 2 * order), jnp.float32)],
        name="factor",
    )(packed)
    return inverse, upper, spread.reshape(())


def apply_kernel(tiles_ref, inverse_ref, rows_ref, buffer, done):
    order = inverse_ref.shape[0]
    blocks = done.shape[0]
    high, middle, low = split(jnp.transpose(inverse_ref[...]))
    double = jnp.concatenate([high, middle], axis=1)
    double = jnp.concatenate([double, double], axis=0)
    single = jnp.concatenate([low, high], axis=0)
    copies = []
    for block in range(blocks):
        values = jnp.transpose(tiles_ref[pl.ds(block, order, stride=blocks), :])
        high, middle, low = split(values)
        most = bf16_product(jnp.concatenate([high, middle], axis=1), double)
        rest = bf16_product(jnp.concatenate([high, low], axis=1), single)
        part = pl.ds(block * LANES, LANES)
        buffer[part, :] = most[:, :order] + (most[:, order:] + rest)
        copies.append(
            pltpu.make_async_copy(buffer.at[part, :], rows_ref.at[part, :], done.at[block])
        )
        copies[-1].start()
    for copy in copies:
        copy.wait()


def apply(tiles, inverse):
    order = inverse.shape[0]
    blocks = tiles.shape[0] // order
    whole = pl.BlockSpec(memory_space=pltpu.VMEM)
    return pl.pallas_call(
        apply_kernel,
        out_shape=jax.ShapeDtypeStruct((blocks * LANES, order), jnp.float32),
        in_specs=[whole, whole],
        out_specs=pl.BlockSpec(memory_space=pl.ANY),
        scratch_shapes=[
            pltpu.VMEM((blocks * LANES, order), jnp.float32),
            pltpu.SemaphoreType.DMA((blocks,)),
        ],
        name="apply",
    )(tiles, inverse)


def shards(snapshots):
    held, length = snapshots.shape
    groups = lax.axis_size("wide")
    tiles = length // LANES
    blocks = snapshots.reshape(held, tiles, LANES).transpose(1, 0, 2)
    blocks = exchange(blocks, "wide").reshape(groups, tiles // groups, held, LANES)
    tiles = blocks.transpose(0, 2, 1, 3).reshape(-1, LANES)
    columns = tiles.reshape(groups * held, length // groups)

    root = math.sqrt(length * lax.axis_size("narrow"))

    inverse, upper, spread = factor(total(gram(columns, 1)), root)

    def rough(state):
        return state[2] > LIMIT

    def again(state):
        inverse, upper, spread = state
        more, next_upper, fresh = factor(total(gram(apply(tiles, inverse), 0)), root)
        fresh = jnp.minimum(fresh, spread / GAIN)
        return product(more, inverse), product(next_upper, upper), fresh

    inverse, upper, _ = lax.while_loop(rough, again, (inverse, upper, spread))
    return apply(tiles, inverse), upper


def solution(mesh):
    in_specs = (P("wide", "narrow"),)
    out_specs = (P(("narrow", "wide"), None), P())
    return jax.shard_map(shards, mesh=mesh, in_specs=in_specs, out_specs=out_specs, check_vma=False)
```

```python
import functools
import math

import jax
import jax.numpy as jnp
import numpy as np
from jax import lax
from jax.experimental import pallas as pl
from jax.experimental.pallas import tpu as pltpu
from jax.sharding import PartitionSpec as P

LANES = 128
SUBLANES = 8
PANEL = 16
FLOOR = 1e-6
LIMIT = 4096.0
CAP = 1e9
GAIN = 64.0


def product(left, right, dims=((1,), (0,))):
    return lax.dot_general(
        left,
        right,
        (dims, ((), ())),
        precision=lax.Precision.HIGHEST,
        preferred_element_type=jnp.float32,
    )


def exchange(pieces, axis, groups=None):
    return lax.all_to_all(
        pieces, axis, split_axis=0, concat_axis=0, axis_index_groups=groups, tiled=True
    )


EVERY = ("wide", "narrow")


def added(part, groups):
    pieces = jnp.broadcast_to(part, (len(groups[0]), *part.shape))
    return jnp.sum(exchange(pieces, EVERY, groups), axis=0)


def paired(part, groups):
    return lax.all_gather(part, EVERY, axis_index_groups=groups)


def total(packed):
    wide, narrow = lax.axis_size("wide"), lax.axis_size("narrow")
    side = math.isqrt(wide)
    places = np.arange(wide * narrow).reshape(side // 2, 2, side // 2, 2, narrow // 2, 2)
    pairs = places.reshape(-1, 2).tolist()
    even, odd = places[..., 0], places[..., 1]
    first = [even.transpose(0, 1, 3, 4, 2), odd.transpose(1, 2, 3, 4, 0)]
    second = [even.transpose(2, 4, 3, 0, 1), odd.transpose(0, 4, 1, 2, 3)]
    first = np.concatenate([part.reshape(-1, narrow // 2 * (side // 2)) for part in first])
    second = np.concatenate([part.reshape(-1, 2 * side) for part in second])
    half = packed.shape[0] // 2
    both = jnp.sum(paired(packed, pairs), axis=0)
    part = lax.dynamic_slice_in_dim(both, lax.axis_index("narrow") % 2 * half, half, axis=0)
    part = part.reshape(1, -1)
    part = added(part, first.tolist())
    part = added(part, second.tolist())
    return paired(part.reshape(half, -1), pairs)


def gram(values, dim):
    square = product(values, values, ((dim,), (dim,)))
    half = square.shape[0] // 2
    across = lax.broadcasted_iota(jnp.int32, (half, 2 * half), 1)
    down = lax.broadcasted_iota(jnp.int32, (half, 2 * half), 0)
    bottom = square[half:, :]
    rows = jnp.where(across < down, jnp.roll(bottom, half, axis=1), square[:half, :])
    corner = jnp.sum(jnp.where(across == down + half, bottom, 0.0), axis=0, keepdims=True)
    return jnp.concatenate([rows, jnp.broadcast_to(corner, (2, 2 * half))], axis=0)


def split(value):
    high = value.astype(jnp.bfloat16)
    rest = value - high.astype(jnp.float32)
    middle = rest.astype(jnp.bfloat16)
    low = (rest - middle.astype(jnp.float32)).astype(jnp.bfloat16)
    return high, middle, low


def bf16_product(left, right):
    return jnp.dot(left, right, preferred_element_type=jnp.float32)


def replicated(value):
    return jnp.broadcast_to(value, (SUBLANES, LANES))


def stacked(values):
    place = lax.broadcasted_iota(jnp.int32, (SUBLANES, LANES), 0)
    blocks = []
    for first in range(0, len(values), SUBLANES):
        block = values[first]
        for step in range(1, SUBLANES):
            block = jnp.where(place == step, values[first + step], block)
        blocks.append(block)
    return jnp.concatenate(blocks, axis=0)


def factor_kernel(root, packed_ref, inverse_ref, upper_ref, spread_ref, work):
    order = packed_ref.shape[2]
    half = order // 2
    rows = packed_ref.shape[1]
    across = lax.broadcasted_iota(jnp.int32, (order, order), 1)
    down = lax.broadcasted_iota(jnp.int32, (order, order), 0)
    top = jnp.concatenate([packed_ref[0], packed_ref[1, : half - rows]], axis=0)
    corner = packed_ref[1, half - rows : half - rows + 1]
    flipped = pltpu.roll(jnp.transpose(jnp.concatenate([top, top], axis=0))[:half, :], half, 1)
    bottom = jnp.where((across == down + half)[:half, :], corner, flipped)
    gram = jnp.concatenate([top, bottom], axis=0)
    diagonal = jnp.where(across == down, gram, 0.0)
    scale = lax.rsqrt(jnp.sum(diagonal, axis=0, keepdims=True))
    work[:, :order] = gram * scale * lax.rsqrt(jnp.sum(diagonal, axis=1, keepdims=True))
    work[:, order:] = jnp.where(across == down, 1.0, 0.0)
    for base in range(0, order, PANEL):
        end = base + PANEL
        panel = work[base:end, :order]
        entry = {}
        for col in range(PANEL):
            lanes = jnp.full(panel.shape, base + col, jnp.int32)
            spread_col = jnp.take_along_axis(panel, lanes, axis=1)
            for row in range(col + 1):
                entry[row, col] = replicated(spread_col[row : row + 1, :])
        left = [replicated(work[base + row : base + row + 1, :order]) for row in range(PANEL)]
        right = [replicated(work[base + row : base + row + 1, order:]) for row in range(PANEL)]
        for pivot in range(PANEL):
            inv = lax.rsqrt(jnp.maximum(entry[pivot, pivot], FLOOR))
            left[pivot] = left[pivot] * inv
            right[pivot] = right[pivot] * inv
            for col in range(pivot + 1, PANEL):
                entry[pivot, col] = entry[pivot, col] * inv
            for col in range(pivot + 1, PANEL):
                ratio = entry[pivot, col]
                for row in range(pivot + 1, col + 1):
                    entry[row, col] = entry[row, col] - entry[pivot, row] * ratio
                left[col] = left[col] - ratio * left[pivot]
                right[col] = right[col] - ratio * right[pivot]
        rows = jnp.concatenate([stacked(left), stacked(right)], axis=1)
        work[base:end, :] = rows
        if end < order:
            high, middle, low = split(rows)
            first = jnp.concatenate([high, high, middle, high, low, middle], axis=0)
            second = jnp.concatenate([high, middle, high, low, high, middle], axis=0)
            update = lax.dot_general(
                first[:, :order],
                second,
                (((0,), (0,)), ((), ())),
                preferred_element_type=jnp.float32,
            )
            work[end:, :] -= update[end:, :]
    inverse = jnp.where(across <= down, work[:, order:], 0.0)
    spread_ref[...] = jnp.minimum(jnp.sum(inverse * inverse, keepdims=True), CAP)
    inverse_ref[...] = inverse * (scale * root)
    upper_ref[...] = jnp.where(across >= down, work[:, :order], 0.0) * (1.0 / (scale * root))


def factor(packed, root):
    order = packed.shape[2]
    shape = jax.ShapeDtypeStruct((order, order), jnp.float32)
    whole = pl.BlockSpec(memory_space=pltpu.VMEM)
    inverse, upper, spread = pl.pallas_call(
        functools.partial(factor_kernel, root),
        out_shape=[shape, shape, jax.ShapeDtypeStruct((1, 1), jnp.float32)],
        in_specs=[whole],
        out_specs=[whole] * 3,
        scratch_shapes=[pltpu.VMEM((order, 2 * order), jnp.float32)],
        name="factor",
    )(packed)
    return inverse, upper, spread.reshape(())


def apply_kernel(tiles_ref, inverse_ref, rows_ref, buffer, done):
    order = inverse_ref.shape[0]
    blocks = done.shape[0]
    high, middle, low = split(jnp.transpose(inverse_ref[...]))
    double = jnp.concatenate([high, middle], axis=1)
    double = jnp.concatenate([double, double], axis=0)
    single = jnp.concatenate([low, high], axis=0)
    copies = []
    for block in range(blocks):
        values = jnp.transpose(tiles_ref[pl.ds(block, order, stride=blocks), :])
        high, middle, low = split(values)
        most = bf16_product(jnp.concatenate([high, middle], axis=1), double)
        rest = bf16_product(jnp.concatenate([high, low], axis=1), single)
        part = pl.ds(block * LANES, LANES)
        buffer[part, :] = most[:, :order] + (most[:, order:] + rest)
        copies.append(
            pltpu.make_async_copy(buffer.at[part, :], rows_ref.at[part, :], done.at[block])
        )
        copies[-1].start()
    for copy in copies:
        copy.wait()


def apply(tiles, inverse):
    order = inverse.shape[0]
    blocks = tiles.shape[0] // order
    whole = pl.BlockSpec(memory_space=pltpu.VMEM)
    return pl.pallas_call(
        apply_kernel,
        out_shape=jax.ShapeDtypeStruct((blocks * LANES, order), jnp.float32),
        in_specs=[whole, whole],
        out_specs=pl.BlockSpec(memory_space=pl.ANY),
        scratch_shapes=[
            pltpu.VMEM((blocks * LANES, order), jnp.float32),
            pltpu.SemaphoreType.DMA((blocks,)),
        ],
        name="apply",
    )(tiles, inverse)


def shards(snapshots):
    held, length = snapshots.shape
    groups = lax.axis_size("wide")
    tiles = length // LANES
    blocks = snapshots.reshape(held, tiles, LANES).transpose(1, 0, 2)
    blocks = exchange(blocks, "wide").reshape(groups, tiles // groups, held, LANES)
    tiles = blocks.transpose(0, 2, 1, 3).reshape(-1, LANES)
    columns = tiles.reshape(groups * held, length // groups)

    root = math.sqrt(length * lax.axis_size("narrow"))

    inverse, upper, spread = factor(total(gram(columns, 1)), root)

    def rough(state):
        return state[2] > LIMIT

    def again(state):
        inverse, upper, spread = state
        more, next_upper, fresh = factor(total(gram(apply(tiles, inverse), 0)), root)
        fresh = jnp.minimum(fresh, spread / GAIN)
        return product(more, inverse), product(next_upper, upper), fresh

    inverse, upper, _ = lax.while_loop(rough, again, (inverse, upper, spread))
    return apply(tiles, inverse), upper


def solution(mesh):
    in_specs = (P("wide", "narrow"),)
    out_specs = (P(("narrow", "wide"), None), P())
    return jax.shard_map(shards, mesh=mesh, in_specs=in_specs, out_specs=out_specs, check_vma=False)
```

```python
import functools
import math

import jax
import jax.numpy as jnp
import numpy as np
from jax import lax
from jax.experimental import pallas as pl
from jax.experimental.pallas import tpu as pltpu
from jax.sharding import PartitionSpec as P

LANES = 128
SUBLANES = 8
PANEL = 16
FLOOR = 1e-6
LIMIT = 4096.0
CAP = 1e9
GAIN = 64.0


def product(left, right, dims=((1,), (0,))):
    return lax.dot_general(
        left,
        right,
        (dims, ((), ())),
        precision=lax.Precision.HIGHEST,
        preferred_element_type=jnp.float32,
    )


def exchange(pieces, axis, groups=None):
    return lax.all_to_all(
        pieces, axis, split_axis=0, concat_axis=0, axis_index_groups=groups, tiled=True
    )


EVERY = ("wide", "narrow")


def added(part, groups):
    pieces = jnp.broadcast_to(part, (len(groups[0]), *part.shape))
    return jnp.sum(exchange(pieces, EVERY, groups), axis=0)


def paired(part, groups):
    return lax.all_gather(part, EVERY, axis_index_groups=groups)


def total(packed):
    wide, narrow = lax.axis_size("wide"), lax.axis_size("narrow")
    side = math.isqrt(wide)
    places = np.arange(wide * narrow).reshape(side // 2, 2, side // 2, 2, narrow // 2, 2)
    pairs = places.reshape(-1, 2).tolist()
    first = places.transpose(5, 0, 1, 3, 4, 2).reshape(-1, narrow // 2 * (side // 2))
    second = places.transpose(5, 2, 4, 3, 0, 1).reshape(-1, 2 * side)
    half = packed.shape[0] // 2
    both = jnp.sum(paired(packed, pairs), axis=0)
    part = lax.dynamic_slice_in_dim(both, lax.axis_index("narrow") % 2 * half, half, axis=0)
    part = part.reshape(1, -1)
    part = added(part, first.tolist())
    part = added(part, second.tolist())
    return paired(part.reshape(half, -1), pairs)


def gram(values, dim):
    square = product(values, values, ((dim,), (dim,)))
    half = square.shape[0] // 2
    across = lax.broadcasted_iota(jnp.int32, (half, 2 * half), 1)
    down = lax.broadcasted_iota(jnp.int32, (half, 2 * half), 0)
    bottom = square[half:, :]
    rows = jnp.where(across < down, jnp.roll(bottom, half, axis=1), square[:half, :])
    corner = jnp.sum(jnp.where(across == down + half, bottom, 0.0), axis=0, keepdims=True)
    return jnp.concatenate([rows, jnp.broadcast_to(corner, (2, 2 * half))], axis=0)


def split(value):
    high = value.astype(jnp.bfloat16)
    rest = value - high.astype(jnp.float32)
    middle = rest.astype(jnp.bfloat16)
    low = (rest - middle.astype(jnp.float32)).astype(jnp.bfloat16)
    return high, middle, low


def bf16_product(left, right):
    return jnp.dot(left, right, preferred_element_type=jnp.float32)


def replicated(value):
    return jnp.broadcast_to(value, (SUBLANES, LANES))


def stacked(values):
    place = lax.broadcasted_iota(jnp.int32, (SUBLANES, LANES), 0)
    blocks = []
    for first in range(0, len(values), SUBLANES):
        block = values[first]
        for step in range(1, SUBLANES):
            block = jnp.where(place == step, values[first + step], block)
        blocks.append(block)
    return jnp.concatenate(blocks, axis=0)


def factor_kernel(root, packed_ref, inverse_ref, upper_ref, spread_ref, work):
    order = packed_ref.shape[2]
    half = order // 2
    rows = packed_ref.shape[1]
    across = lax.broadcasted_iota(jnp.int32, (order, order), 1)
    down = lax.broadcasted_iota(jnp.int32, (order, order), 0)
    top = jnp.concatenate([packed_ref[0], packed_ref[1, : half - rows]], axis=0)
    corner = packed_ref[1, half - rows : half - rows + 1]
    flipped = pltpu.roll(jnp.transpose(jnp.concatenate([top, top], axis=0))[:half, :], half, 1)
    bottom = jnp.where((across == down + half)[:half, :], corner, flipped)
    gram = jnp.concatenate([top, bottom], axis=0)
    diagonal = jnp.where(across == down, gram, 0.0)
    scale = lax.rsqrt(jnp.sum(diagonal, axis=0, keepdims=True))
    work[:, :order] = gram * scale * lax.rsqrt(jnp.sum(diagonal, axis=1, keepdims=True))
    work[:, order:] = jnp.where(across == down, 1.0, 0.0)
    for base in range(0, order, PANEL):
        end = base + PANEL
        panel = work[base:end, :order]
        entry = {}
        for col in range(PANEL):
            lanes = jnp.full(panel.shape, base + col, jnp.int32)
            spread_col = jnp.take_along_axis(panel, lanes, axis=1)
            for row in range(col + 1):
                entry[row, col] = replicated(spread_col[row : row + 1, :])
        left = [replicated(work[base + row : base + row + 1, :order]) for row in range(PANEL)]
        right = [replicated(work[base + row : base + row + 1, order:]) for row in range(PANEL)]
        for pivot in range(PANEL):
            inv = lax.rsqrt(jnp.maximum(entry[pivot, pivot], FLOOR))
            left[pivot] = left[pivot] * inv
            right[pivot] = right[pivot] * inv
            for col in range(pivot + 1, PANEL):
                entry[pivot, col] = entry[pivot, col] * inv
            for col in range(pivot + 1, PANEL):
                ratio = entry[pivot, col]
                for row in range(pivot + 1, col + 1):
                    entry[row, col] = entry[row, col] - entry[pivot, row] * ratio
                left[col] = left[col] - ratio * left[pivot]
                right[col] = right[col] - ratio * right[pivot]
        rows = jnp.concatenate([stacked(left), stacked(right)], axis=1)
        work[base:end, :] = rows
        if end < order:
            high, middle, low = split(rows)
            first = jnp.concatenate([high, high, middle, high, low, middle], axis=0)
            second = jnp.concatenate([high, middle, high, low, high, middle], axis=0)
            update = lax.dot_general(
                first[:, :order],
                second,
                (((0,), (0,)), ((), ())),
                preferred_element_type=jnp.float32,
            )
            work[end:, :] -= update[end:, :]
    inverse = jnp.where(across <= down, work[:, order:], 0.0)
    spread_ref[...] = jnp.minimum(jnp.sum(inverse * inverse, keepdims=True), CAP)
    inverse_ref[...] = inverse * (scale * root)
    upper_ref[...] = jnp.where(across >= down, work[:, :order], 0.0) * (1.0 / (scale * root))


def factor(packed, root):
    order = packed.shape[2]
    shape = jax.ShapeDtypeStruct((order, order), jnp.float32)
    whole = pl.BlockSpec(memory_space=pltpu.VMEM)
    inverse, upper, spread = pl.pallas_call(
        functools.partial(factor_kernel, root),
        out_shape=[shape, shape, jax.ShapeDtypeStruct((1, 1), jnp.float32)],
        in_specs=[whole],
        out_specs=[whole] * 3,
        scratch_shapes=[pltpu.VMEM((order, 2 * order), jnp.float32)],
        compiler_params=pltpu.CompilerParams(vmem_limit_bytes=8 * 1024 * 1024),
        name="factor",
    )(packed)
    return inverse, upper, spread.reshape(())


def apply_kernel(tiles_ref, inverse_ref, rows_ref, buffer, done):
    order = inverse_ref.shape[0]
    blocks = done.shape[0]
    high, middle, low = split(jnp.transpose(inverse_ref[...]))
    double = jnp.concatenate([high, middle], axis=1)
    double = jnp.concatenate([double, double], axis=0)
    single = jnp.concatenate([low, high], axis=0)
    copies = []
    for block in range(blocks):
        values = jnp.transpose(tiles_ref[pl.ds(block, order, stride=blocks), :])
        high, middle, low = split(values)
        most = bf16_product(jnp.concatenate([high, middle], axis=1), double)
        rest = bf16_product(jnp.concatenate([high, low], axis=1), single)
        part = pl.ds(block * LANES, LANES)
        buffer[part, :] = most[:, :order] + (most[:, order:] + rest)
        copies.append(
            pltpu.make_async_copy(buffer.at[part, :], rows_ref.at[part, :], done.at[block])
        )
        copies[-1].start()
    for copy in copies:
        copy.wait()


def apply(tiles, inverse):
    order = inverse.shape[0]
    blocks = tiles.shape[0] // order
    whole = pl.BlockSpec(memory_space=pltpu.VMEM)
    return pl.pallas_call(
        apply_kernel,
        out_shape=jax.ShapeDtypeStruct((blocks * LANES, order), jnp.float32),
        in_specs=[whole, whole],
        out_specs=pl.BlockSpec(memory_space=pl.ANY),
        scratch_shapes=[
            pltpu.VMEM((blocks * LANES, order), jnp.float32),
            pltpu.SemaphoreType.DMA((blocks,)),
        ],
        compiler_params=pltpu.CompilerParams(vmem_limit_bytes=8 * 1024 * 1024),
        name="apply",
    )(tiles, inverse)


def shards(snapshots):
    held, length = snapshots.shape
    groups = lax.axis_size("wide")
    tiles = length // LANES
    blocks = snapshots.reshape(held, tiles, LANES).transpose(1, 0, 2)
    blocks = exchange(blocks, "wide").reshape(groups, tiles // groups, held, LANES)
    tiles = blocks.transpose(0, 2, 1, 3).reshape(-1, LANES)
    columns = tiles.reshape(groups * held, length // groups)

    root = math.sqrt(length * lax.axis_size("narrow"))

    inverse, upper, spread = factor(total(gram(columns, 1)), root)

    def rough(state):
        return state[2] > LIMIT

    def again(state):
        inverse, upper, spread = state
        more, next_upper, fresh = factor(total(gram(apply(tiles, inverse), 0)), root)
        fresh = jnp.minimum(fresh, spread / GAIN)
        return product(more, inverse), product(next_upper, upper), fresh

    inverse, upper, _ = lax.while_loop(rough, again, (inverse, upper, spread))
    return apply(tiles, inverse), upper


def solution(mesh):
    in_specs = (P("wide", "narrow"),)
    out_specs = (P(("narrow", "wide"), None), P())
    return jax.shard_map(shards, mesh=mesh, in_specs=in_specs, out_specs=out_specs, check_vma=False)
```

```python
import functools
import math

import jax
import jax.numpy as jnp
import numpy as np
from jax import lax
from jax.experimental import pallas as pl
from jax.experimental.pallas import tpu as pltpu
from jax.sharding import PartitionSpec as P

LANES = 128
SUBLANES = 8
PANEL = 16
FLOOR = 1e-6
LIMIT = 4096.0
CAP = 1e9
GAIN = 64.0
VMEM_LIMIT = 8 * 1024 * 1024


def product(left, right, dims=((1,), (0,))):
    return lax.dot_general(
        left,
        right,
        (dims, ((), ())),
        precision=lax.Precision.HIGHEST,
        preferred_element_type=jnp.float32,
    )


def exchange(pieces, axis, groups=None):
    return lax.all_to_all(
        pieces, axis, split_axis=0, concat_axis=0, axis_index_groups=groups, tiled=True
    )


EVERY = ("wide", "narrow")


def added(part, groups):
    pieces = jnp.broadcast_to(part, (len(groups[0]), *part.shape))
    return jnp.sum(exchange(pieces, EVERY, groups), axis=0)


def paired(part, groups):
    return lax.all_gather(part, EVERY, axis_index_groups=groups)


def total(packed):
    wide, narrow = lax.axis_size("wide"), lax.axis_size("narrow")
    side = math.isqrt(wide)
    places = np.arange(wide * narrow).reshape(side // 2, 2, side // 2, 2, narrow // 2, 2)
    pairs = places.reshape(-1, 2).tolist()
    even, odd = places[..., 0], places[..., 1]
    first = [even.transpose(0, 1, 3, 4, 2), odd.transpose(1, 2, 3, 4, 0)]
    second = [even.transpose(2, 4, 3, 0, 1), odd.transpose(0, 4, 1, 2, 3)]
    first = np.concatenate([part.reshape(-1, narrow // 2 * (side // 2)) for part in first])
    second = np.concatenate([part.reshape(-1, 2 * side) for part in second])
    half = packed.shape[0] // 2
    both = jnp.sum(paired(packed, pairs), axis=0)
    part = lax.dynamic_slice_in_dim(both, lax.axis_index("narrow") % 2 * half, half, axis=0)
    part = part.reshape(1, -1)
    part = added(part, first.tolist())
    part = added(part, second.tolist())
    return paired(part.reshape(half, -1), pairs)


def gram(values, dim):
    square = product(values, values, ((dim,), (dim,)))
    half = square.shape[0] // 2
    across = lax.broadcasted_iota(jnp.int32, (half, 2 * half), 1)
    down = lax.broadcasted_iota(jnp.int32, (half, 2 * half), 0)
    bottom = square[half:, :]
    rows = jnp.where(across < down, jnp.roll(bottom, half, axis=1), square[:half, :])
    corner = jnp.sum(jnp.where(across == down + half, bottom, 0.0), axis=0, keepdims=True)
    return jnp.concatenate([rows, jnp.broadcast_to(corner, (2, 2 * half))], axis=0)


def split(value):
    high = value.astype(jnp.bfloat16)
    rest = value - high.astype(jnp.float32)
    middle = rest.astype(jnp.bfloat16)
    low = (rest - middle.astype(jnp.float32)).astype(jnp.bfloat16)
    return high, middle, low


def bf16_product(left, right):
    return jnp.dot(left, right, preferred_element_type=jnp.float32)


def replicated(value):
    return jnp.broadcast_to(value, (SUBLANES, LANES))


def stacked(values):
    place = lax.broadcasted_iota(jnp.int32, (SUBLANES, LANES), 0)
    blocks = []
    for first in range(0, len(values), SUBLANES):
        block = values[first]
        for step in range(1, SUBLANES):
            block = jnp.where(place == step, values[first + step], block)
        blocks.append(block)
    return jnp.concatenate(blocks, axis=0)


def factor_kernel(root, packed_ref, inverse_ref, upper_ref, spread_ref, work):
    order = packed_ref.shape[2]
    half = order // 2
    rows = packed_ref.shape[1]
    across = lax.broadcasted_iota(jnp.int32, (order, order), 1)
    down = lax.broadcasted_iota(jnp.int32, (order, order), 0)
    top = jnp.concatenate([packed_ref[0], packed_ref[1, : half - rows]], axis=0)
    corner = packed_ref[1, half - rows : half - rows + 1]
    flipped = pltpu.roll(jnp.transpose(jnp.concatenate([top, top], axis=0))[:half, :], half, 1)
    bottom = jnp.where((across == down + half)[:half, :], corner, flipped)
    gram = jnp.concatenate([top, bottom], axis=0)
    diagonal = jnp.where(across == down, gram, 0.0)
    scale = lax.rsqrt(jnp.sum(diagonal, axis=0, keepdims=True))
    work[:, :order] = gram * scale * lax.rsqrt(jnp.sum(diagonal, axis=1, keepdims=True))
    work[:, order:] = jnp.where(across == down, 1.0, 0.0)
    for base in range(0, order, PANEL):
        end = base + PANEL
        panel = work[base:end, :order]
        entry = {}
        for col in range(PANEL):
            lanes = jnp.full(panel.shape, base + col, jnp.int32)
            spread_col = jnp.take_along_axis(panel, lanes, axis=1)
            for row in range(col + 1):
                entry[row, col] = replicated(spread_col[row : row + 1, :])
        left = [replicated(work[base + row : base + row + 1, :order]) for row in range(PANEL)]
        right = [replicated(work[base + row : base + row + 1, order:]) for row in range(PANEL)]
        for pivot in range(PANEL):
            inv = lax.rsqrt(jnp.maximum(entry[pivot, pivot], FLOOR))
            left[pivot] = left[pivot] * inv
            right[pivot] = right[pivot] * inv
            for col in range(pivot + 1, PANEL):
                entry[pivot, col] = entry[pivot, col] * inv
            for col in range(pivot + 1, PANEL):
                ratio = entry[pivot, col]
                for row in range(pivot + 1, col + 1):
                    entry[row, col] = entry[row, col] - entry[pivot, row] * ratio
                left[col] = left[col] - ratio * left[pivot]
                right[col] = right[col] - ratio * right[pivot]
        rows = jnp.concatenate([stacked(left), stacked(right)], axis=1)
        work[base:end, :] = rows
        if end < order:
            high, middle, low = split(rows)
            first = jnp.concatenate([high, high, middle, high, low, middle], axis=0)
            second = jnp.concatenate([high, middle, high, low, high, middle], axis=0)
            update = lax.dot_general(
                first[:, :order],
                second,
                (((0,), (0,)), ((), ())),
                preferred_element_type=jnp.float32,
            )
            work[end:, :] -= update[end:, :]
    inverse = jnp.where(across <= down, work[:, order:], 0.0)
    spread_ref[...] = jnp.minimum(jnp.sum(inverse * inverse, keepdims=True), CAP)
    inverse_ref[...] = inverse * (scale * root)
    upper_ref[...] = jnp.where(across >= down, work[:, :order], 0.0) * (1.0 / (scale * root))


def factor(packed, root):
    order = packed.shape[2]
    shape = jax.ShapeDtypeStruct((order, order), jnp.float32)
    whole = pl.BlockSpec(memory_space=pltpu.VMEM)
    inverse, upper, spread = pl.pallas_call(
        functools.partial(factor_kernel, root),
        out_shape=[shape, shape, jax.ShapeDtypeStruct((1, 1), jnp.float32)],
        in_specs=[whole],
        out_specs=[whole] * 3,
        scratch_shapes=[pltpu.VMEM((order, 2 * order), jnp.float32)],
        compiler_params=pltpu.CompilerParams(vmem_limit_bytes=VMEM_LIMIT),
        name="factor",
    )(packed)
    return inverse, upper, spread.reshape(())


def apply_kernel(tiles_ref, inverse_ref, rows_ref, buffer, done):
    order = inverse_ref.shape[0]
    blocks = done.shape[0]
    high, middle, low = split(jnp.transpose(inverse_ref[...]))
    double = jnp.concatenate([high, middle], axis=1)
    double = jnp.concatenate([double, double], axis=0)
    single = jnp.concatenate([low, high], axis=0)
    copies = []
    for block in range(blocks):
        values = jnp.transpose(tiles_ref[pl.ds(block, order, stride=blocks), :])
        high, middle, low = split(values)
        most = bf16_product(jnp.concatenate([high, middle], axis=1), double)
        rest = bf16_product(jnp.concatenate([high, low], axis=1), single)
        part = pl.ds(block * LANES, LANES)
        buffer[part, :] = most[:, :order] + (most[:, order:] + rest)
        copies.append(
            pltpu.make_async_copy(buffer.at[part, :], rows_ref.at[part, :], done.at[block])
        )
        copies[-1].start()
    for copy in copies:
        copy.wait()


def apply(tiles, inverse):
    order = inverse.shape[0]
    blocks = tiles.shape[0] // order
    whole = pl.BlockSpec(memory_space=pltpu.VMEM)
    return pl.pallas_call(
        apply_kernel,
        out_shape=jax.ShapeDtypeStruct((blocks * LANES, order), jnp.float32),
        in_specs=[whole, whole],
        out_specs=pl.BlockSpec(memory_space=pl.ANY),
        scratch_shapes=[
            pltpu.VMEM((blocks * LANES, order), jnp.float32),
            pltpu.SemaphoreType.DMA((blocks,)),
        ],
        compiler_params=pltpu.CompilerParams(vmem_limit_bytes=VMEM_LIMIT),
        name="apply",
    )(tiles, inverse)


def shards(snapshots):
    held, length = snapshots.shape
    groups = lax.axis_size("wide")
    tiles = length // LANES
    blocks = snapshots.reshape(held, tiles, LANES).transpose(1, 0, 2)
    blocks = exchange(blocks, "wide").reshape(groups, tiles // groups, held, LANES)
    tiles = blocks.transpose(0, 2, 1, 3).reshape(-1, LANES)
    columns = tiles.reshape(groups * held, length // groups)

    root = math.sqrt(length * lax.axis_size("narrow"))

    inverse, upper, spread = factor(total(gram(columns, 1)), root)

    def rough(state):
        return state[2] > LIMIT

    def again(state):
        inverse, upper, spread = state
        more, next_upper, fresh = factor(total(gram(apply(tiles, inverse), 0)), root)
        fresh = jnp.minimum(fresh, spread / GAIN)
        return product(more, inverse), product(next_upper, upper), fresh

    inverse, upper, _ = lax.while_loop(rough, again, (inverse, upper, spread))
    return apply(tiles, inverse), upper


def solution(mesh):
    in_specs = (P("wide", "narrow"),)
    out_specs = (P(("narrow", "wide"), None), P())
    return jax.shard_map(shards, mesh=mesh, in_specs=in_specs, out_specs=out_specs, check_vma=False)
```

```python
import functools
import math

import jax
import jax.numpy as jnp
import numpy as np
from jax import lax
from jax.experimental import pallas as pl
from jax.experimental.pallas import tpu as pltpu
from jax.sharding import PartitionSpec as P

LANES = 128
SUBLANES = 8
PANEL = 16
FLOOR = 1e-6
LIMIT = 4096.0
CAP = 1e9
GAIN = 64.0
VMEM_LIMIT = 8 * 1024 * 1024


def product(left, right, dims=((1,), (0,))):
    return lax.dot_general(
        left,
        right,
        (dims, ((), ())),
        precision=lax.Precision.HIGHEST,
        preferred_element_type=jnp.float32,
    )


def exchange(pieces, axis, groups=None):
    return lax.all_to_all(
        pieces, axis, split_axis=0, concat_axis=0, axis_index_groups=groups, tiled=True
    )


EVERY = ("wide", "narrow")


def added(part, groups):
    pieces = jnp.broadcast_to(part, (len(groups[0]), *part.shape))
    return jnp.sum(exchange(pieces, EVERY, groups), axis=0)


def paired(part, groups):
    return lax.all_gather(part, EVERY, axis_index_groups=groups)


def total(packed):
    wide, narrow = lax.axis_size("wide"), lax.axis_size("narrow")
    side = math.isqrt(wide)
    places = np.arange(wide * narrow).reshape(side // 2, 2, side // 2, 2, narrow // 2, 2)
    pairs = places.reshape(-1, 2).tolist()
    even, odd = places[..., 0], places[..., 1]
    first = [even.transpose(2, 4, 3, 0, 1), odd.transpose(0, 4, 1, 2, 3)]
    second = [even.transpose(0, 1, 3, 4, 2), odd.transpose(1, 2, 3, 4, 0)]
    first = np.concatenate([part.reshape(-1, 2 * side) for part in first])
    second = np.concatenate([part.reshape(-1, narrow // 2 * (side // 2)) for part in second])
    half = packed.shape[0] // 2
    both = jnp.sum(paired(packed, pairs), axis=0)
    part = lax.dynamic_slice_in_dim(both, lax.axis_index("narrow") % 2 * half, half, axis=0)
    part = part.reshape(1, -1)
    part = added(part, first.tolist())
    part = added(part, second.tolist())
    return paired(part.reshape(half, -1), pairs)


def gram(values, dim):
    square = product(values, values, ((dim,), (dim,)))
    half = square.shape[0] // 2
    across = lax.broadcasted_iota(jnp.int32, (half, 2 * half), 1)
    down = lax.broadcasted_iota(jnp.int32, (half, 2 * half), 0)
    bottom = square[half:, :]
    rows = jnp.where(across < down, jnp.roll(bottom, half, axis=1), square[:half, :])
    corner = jnp.sum(jnp.where(across == down + half, bottom, 0.0), axis=0, keepdims=True)
    return jnp.concatenate([rows, jnp.broadcast_to(corner, (2, 2 * half))], axis=0)


def split(value):
    high = value.astype(jnp.bfloat16)
    rest = value - high.astype(jnp.float32)
    middle = rest.astype(jnp.bfloat16)
    low = (rest - middle.astype(jnp.float32)).astype(jnp.bfloat16)
    return high, middle, low


def bf16_product(left, right):
    return jnp.dot(left, right, preferred_element_type=jnp.float32)


def replicated(value):
    return jnp.broadcast_to(value, (SUBLANES, LANES))


def stacked(values):
    place = lax.broadcasted_iota(jnp.int32, (SUBLANES, LANES), 0)
    blocks = []
    for first in range(0, len(values), SUBLANES):
        block = values[first]
        for step in range(1, SUBLANES):
            block = jnp.where(place == step, values[first + step], block)
        blocks.append(block)
    return jnp.concatenate(blocks, axis=0)


def factor_kernel(root, packed_ref, inverse_ref, upper_ref, spread_ref, work):
    order = packed_ref.shape[2]
    half = order // 2
    rows = packed_ref.shape[1]
    across = lax.broadcasted_iota(jnp.int32, (order, order), 1)
    down = lax.broadcasted_iota(jnp.int32, (order, order), 0)
    top = jnp.concatenate([packed_ref[0], packed_ref[1, : half - rows]], axis=0)
    corner = packed_ref[1, half - rows : half - rows + 1]
    flipped = pltpu.roll(jnp.transpose(jnp.concatenate([top, top], axis=0))[:half, :], half, 1)
    bottom = jnp.where((across == down + half)[:half, :], corner, flipped)
    gram = jnp.concatenate([top, bottom], axis=0)
    diagonal = jnp.where(across == down, gram, 0.0)
    scale = lax.rsqrt(jnp.sum(diagonal, axis=0, keepdims=True))
    work[:, :order] = gram * scale * lax.rsqrt(jnp.sum(diagonal, axis=1, keepdims=True))
    work[:, order:] = jnp.where(across == down, 1.0, 0.0)
    for base in range(0, order, PANEL):
        end = base + PANEL
        panel = work[base:end, :order]
        entry = {}
        for col in range(PANEL):
            lanes = jnp.full(panel.shape, base + col, jnp.int32)
            spread_col = jnp.take_along_axis(panel, lanes, axis=1)
            for row in range(col + 1):
                entry[row, col] = replicated(spread_col[row : row + 1, :])
        left = [replicated(work[base + row : base + row + 1, :order]) for row in range(PANEL)]
        right = [replicated(work[base + row : base + row + 1, order:]) for row in range(PANEL)]
        for pivot in range(PANEL):
            inv = lax.rsqrt(jnp.maximum(entry[pivot, pivot], FLOOR))
            left[pivot] = left[pivot] * inv
            right[pivot] = right[pivot] * inv
            for col in range(pivot + 1, PANEL):
                entry[pivot, col] = entry[pivot, col] * inv
            for col in range(pivot + 1, PANEL):
                ratio = entry[pivot, col]
                for row in range(pivot + 1, col + 1):
                    entry[row, col] = entry[row, col] - entry[pivot, row] * ratio
                left[col] = left[col] - ratio * left[pivot]
                right[col] = right[col] - ratio * right[pivot]
        rows = jnp.concatenate([stacked(left), stacked(right)], axis=1)
        work[base:end, :] = rows
        if end < order:
            high, middle, low = split(rows)
            first = jnp.concatenate([high, high, middle, high, low, middle], axis=0)
            second = jnp.concatenate([high, middle, high, low, high, middle], axis=0)
            update = lax.dot_general(
                first[:, :order],
                second,
                (((0,), (0,)), ((), ())),
                preferred_element_type=jnp.float32,
            )
            work[end:, :] -= update[end:, :]
    inverse = jnp.where(across <= down, work[:, order:], 0.0)
    spread_ref[...] = jnp.minimum(jnp.sum(inverse * inverse, keepdims=True), CAP)
    inverse_ref[...] = inverse * (scale * root)
    upper_ref[...] = jnp.where(across >= down, work[:, :order], 0.0) * (1.0 / (scale * root))


def factor(packed, root):
    order = packed.shape[2]
    shape = jax.ShapeDtypeStruct((order, order), jnp.float32)
    whole = pl.BlockSpec(memory_space=pltpu.VMEM)
    inverse, upper, spread = pl.pallas_call(
        functools.partial(factor_kernel, root),
        out_shape=[shape, shape, jax.ShapeDtypeStruct((1, 1), jnp.float32)],
        in_specs=[whole],
        out_specs=[whole] * 3,
        scratch_shapes=[pltpu.VMEM((order, 2 * order), jnp.float32)],
        compiler_params=pltpu.CompilerParams(vmem_limit_bytes=VMEM_LIMIT),
        name="factor",
    )(packed)
    return inverse, upper, spread.reshape(())


def apply_kernel(tiles_ref, inverse_ref, rows_ref, buffer, done):
    order = inverse_ref.shape[0]
    blocks = done.shape[0]
    high, middle, low = split(jnp.transpose(inverse_ref[...]))
    double = jnp.concatenate([high, middle], axis=1)
    double = jnp.concatenate([double, double], axis=0)
    single = jnp.concatenate([low, high], axis=0)
    copies = []
    for block in range(blocks):
        values = jnp.transpose(tiles_ref[pl.ds(block, order, stride=blocks), :])
        high, middle, low = split(values)
        most = bf16_product(jnp.concatenate([high, middle], axis=1), double)
        rest = bf16_product(jnp.concatenate([high, low], axis=1), single)
        part = pl.ds(block * LANES, LANES)
        buffer[part, :] = most[:, :order] + (most[:, order:] + rest)
        copies.append(
            pltpu.make_async_copy(buffer.at[part, :], rows_ref.at[part, :], done.at[block])
        )
        copies[-1].start()
    for copy in copies:
        copy.wait()


def apply(tiles, inverse):
    order = inverse.shape[0]
    blocks = tiles.shape[0] // order
    whole = pl.BlockSpec(memory_space=pltpu.VMEM)
    return pl.pallas_call(
        apply_kernel,
        out_shape=jax.ShapeDtypeStruct((blocks * LANES, order), jnp.float32),
        in_specs=[whole, whole],
        out_specs=pl.BlockSpec(memory_space=pl.ANY),
        scratch_shapes=[
            pltpu.VMEM((blocks * LANES, order), jnp.float32),
            pltpu.SemaphoreType.DMA((blocks,)),
        ],
        compiler_params=pltpu.CompilerParams(vmem_limit_bytes=VMEM_LIMIT),
        name="apply",
    )(tiles, inverse)


def shards(snapshots):
    held, length = snapshots.shape
    groups = lax.axis_size("wide")
    tiles = length // LANES
    blocks = snapshots.reshape(held, tiles, LANES).transpose(1, 0, 2)
    blocks = exchange(blocks, "wide").reshape(groups, tiles // groups, held, LANES)
    tiles = blocks.transpose(0, 2, 1, 3).reshape(-1, LANES)
    columns = tiles.reshape(groups * held, length // groups)

    root = math.sqrt(length * lax.axis_size("narrow"))

    inverse, upper, spread = factor(total(gram(columns, 1)), root)

    def rough(state):
        return state[2] > LIMIT

    def again(state):
        inverse, upper, spread = state
        more, next_upper, fresh = factor(total(gram(apply(tiles, inverse), 0)), root)
        fresh = jnp.minimum(fresh, spread / GAIN)
        return product(more, inverse), product(next_upper, upper), fresh

    inverse, upper, _ = lax.while_loop(rough, again, (inverse, upper, spread))
    return apply(tiles, inverse), upper


def solution(mesh):
    in_specs = (P("wide", "narrow"),)
    out_specs = (P(("narrow", "wide"), None), P())
    return jax.shard_map(shards, mesh=mesh, in_specs=in_specs, out_specs=out_specs, check_vma=False)
```

```python
import functools
import math

import jax
import jax.numpy as jnp
import numpy as np
from jax import lax
from jax.experimental import pallas as pl
from jax.experimental.pallas import tpu as pltpu
from jax.sharding import PartitionSpec as P

LANES = 128
SUBLANES = 8
PANEL = 16
FLOOR = 1e-6
LIMIT = 4096.0
CAP = 1e9
GAIN = 64.0
VMEM_LIMIT = 8 * 1024 * 1024


def product(left, right, dims=((1,), (0,))):
    return lax.dot_general(
        left,
        right,
        (dims, ((), ())),
        precision=lax.Precision.HIGHEST,
        preferred_element_type=jnp.float32,
    )


def exchange(pieces, axis, groups=None):
    return lax.all_to_all(
        pieces, axis, split_axis=0, concat_axis=0, axis_index_groups=groups, tiled=True
    )


EVERY = ("wide", "narrow")


def added(part, groups):
    pieces = jnp.broadcast_to(part, (len(groups[0]), *part.shape))
    return jnp.sum(exchange(pieces, EVERY, groups), axis=0)


def paired(part, groups):
    return lax.all_gather(part, EVERY, axis_index_groups=groups)


def total(packed):
    wide, narrow = lax.axis_size("wide"), lax.axis_size("narrow")
    side = math.isqrt(wide)
    places = np.arange(wide * narrow).reshape(side // 2, 2, side // 2, 2, narrow // 2, 2)
    pairs = places.reshape(-1, 2).tolist()
    even, odd = places[..., 0], places[..., 1]
    first = [even.transpose(0, 1, 3, 4, 2), odd.transpose(1, 2, 3, 4, 0)]
    second = [even.transpose(2, 4, 3, 0, 1), odd.transpose(0, 4, 1, 2, 3)]
    first = np.concatenate([part.reshape(-1, narrow // 2 * (side // 2)) for part in first])
    second = np.concatenate([part.reshape(-1, 2 * side) for part in second])
    half = packed.shape[0] // 2
    both = jnp.sum(paired(packed, pairs), axis=0)
    part = lax.dynamic_slice_in_dim(both, lax.axis_index("narrow") % 2 * half, half, axis=0)
    part = part.reshape(1, -1)
    part = added(part, first.tolist())
    part = added(part, second.tolist())
    return paired(part.reshape(half, -1), pairs)


def gram(values, dim):
    square = product(values, values, ((dim,), (dim,)))
    half = square.shape[0] // 2
    across = lax.broadcasted_iota(jnp.int32, (half, 2 * half), 1)
    down = lax.broadcasted_iota(jnp.int32, (half, 2 * half), 0)
    bottom = square[half:, :]
    rows = jnp.where(across < down, jnp.roll(bottom, half, axis=1), square[:half, :])
    corner = jnp.sum(jnp.where(across == down + half, bottom, 0.0), axis=0, keepdims=True)
    return jnp.concatenate([rows, jnp.broadcast_to(corner, (2, 2 * half))], axis=0)


def split(value):
    high = value.astype(jnp.bfloat16)
    rest = value - high.astype(jnp.float32)
    middle = rest.astype(jnp.bfloat16)
    low = (rest - middle.astype(jnp.float32)).astype(jnp.bfloat16)
    return high, middle, low


def bf16_product(left, right):
    return jnp.dot(left, right, preferred_element_type=jnp.float32)


def replicated(value):
    return jnp.broadcast_to(value, (SUBLANES, LANES))


def stacked(values):
    place = lax.broadcasted_iota(jnp.int32, (SUBLANES, LANES), 0)
    blocks = []
    for first in range(0, len(values), SUBLANES):
        block = values[first]
        for step in range(1, SUBLANES):
            block = jnp.where(place == step, values[first + step], block)
        blocks.append(block)
    return jnp.concatenate(blocks, axis=0)


def factor_kernel(root, packed_ref, inverse_ref, upper_ref, spread_ref, work):
    order = packed_ref.shape[2]
    half = order // 2
    rows = packed_ref.shape[1]
    across = lax.broadcasted_iota(jnp.int32, (order, order), 1)
    down = lax.broadcasted_iota(jnp.int32, (order, order), 0)
    top = jnp.concatenate([packed_ref[0], packed_ref[1, : half - rows]], axis=0)
    corner = packed_ref[1, half - rows : half - rows + 1]
    flipped = pltpu.roll(jnp.transpose(jnp.concatenate([top, top], axis=0))[:half, :], half, 1)
    bottom = jnp.where((across == down + half)[:half, :], corner, flipped)
    gram = jnp.concatenate([top, bottom], axis=0)
    diagonal = jnp.where(across == down, gram, 0.0)
    scale = lax.rsqrt(jnp.sum(diagonal, axis=0, keepdims=True))
    work[:, :order] = gram * scale * lax.rsqrt(jnp.sum(diagonal, axis=1, keepdims=True))
    work[:, order:] = jnp.where(across == down, 1.0, 0.0)
    for base in range(0, order, PANEL):
        end = base + PANEL
        panel = work[base:end, :order]
        entry = {}
        for col in range(PANEL):
            lanes = jnp.full(panel.shape, base + col, jnp.int32)
            spread_col = jnp.take_along_axis(panel, lanes, axis=1)
            for row in range(col + 1):
                entry[row, col] = replicated(spread_col[row : row + 1, :])
        left = [replicated(work[base + row : base + row + 1, :order]) for row in range(PANEL)]
        right = [replicated(work[base + row : base + row + 1, order:]) for row in range(PANEL)]
        for pivot in range(PANEL):
            inv = lax.rsqrt(jnp.maximum(entry[pivot, pivot], FLOOR))
            left[pivot] = left[pivot] * inv
            right[pivot] = right[pivot] * inv
            for col in range(pivot + 1, PANEL):
                entry[pivot, col] = entry[pivot, col] * inv
            for col in range(pivot + 1, PANEL):
                ratio = entry[pivot, col]
                for row in range(pivot + 1, col + 1):
                    entry[row, col] = entry[row, col] - entry[pivot, row] * ratio
                left[col] = left[col] - ratio * left[pivot]
                right[col] = right[col] - ratio * right[pivot]
        rows = jnp.concatenate([stacked(left), stacked(right)], axis=1)
        work[base:end, :] = rows
        if end < order:
            high, middle, low = split(rows)
            none = jnp.zeros_like(high)
            turned = jnp.concatenate([high, middle, low, high], axis=0)[:, :order]
            turned = jnp.transpose(turned)[end:, :]
            most = jnp.concatenate([high, high, high, none], axis=0)
            rest = jnp.concatenate([middle, middle, none, low], axis=0)
            for side in (slice(0, order), slice(order, 2 * order)):
                both = bf16_product(turned, jnp.concatenate([most[:, side], rest[:, side]], axis=1))
                work[end:, side] -= both[:, :order] + both[:, order:]
    inverse = jnp.where(across <= down, work[:, order:], 0.0)
    spread_ref[...] = jnp.minimum(jnp.sum(inverse * inverse, keepdims=True), CAP)
    inverse_ref[...] = inverse * (scale * root)
    upper_ref[...] = jnp.where(across >= down, work[:, :order], 0.0) * (1.0 / (scale * root))


def factor(packed, root):
    order = packed.shape[2]
    shape = jax.ShapeDtypeStruct((order, order), jnp.float32)
    whole = pl.BlockSpec(memory_space=pltpu.VMEM)
    inverse, upper, spread = pl.pallas_call(
        functools.partial(factor_kernel, root),
        out_shape=[shape, shape, jax.ShapeDtypeStruct((1, 1), jnp.float32)],
        in_specs=[whole],
        out_specs=[whole] * 3,
        scratch_shapes=[pltpu.VMEM((order, 2 * order), jnp.float32)],
        compiler_params=pltpu.CompilerParams(vmem_limit_bytes=VMEM_LIMIT),
        name="factor",
    )(packed)
    return inverse, upper, spread.reshape(())


def apply_kernel(tiles_ref, inverse_ref, rows_ref, buffer, done):
    order = inverse_ref.shape[0]
    blocks = done.shape[0]
    high, middle, low = split(jnp.transpose(inverse_ref[...]))
    double = jnp.concatenate([high, middle], axis=1)
    double = jnp.concatenate([double, double], axis=0)
    single = jnp.concatenate([low, high], axis=0)
    copies = []
    for block in range(blocks):
        values = jnp.transpose(tiles_ref[pl.ds(block, order, stride=blocks), :])
        high, middle, low = split(values)
        most = bf16_product(jnp.concatenate([high, middle], axis=1), double)
        rest = bf16_product(jnp.concatenate([high, low], axis=1), single)
        part = pl.ds(block * LANES, LANES)
        buffer[part, :] = most[:, :order] + (most[:, order:] + rest)
        copies.append(
            pltpu.make_async_copy(buffer.at[part, :], rows_ref.at[part, :], done.at[block])
        )
        copies[-1].start()
    for copy in copies:
        copy.wait()


def apply(tiles, inverse):
    order = inverse.shape[0]
    blocks = tiles.shape[0] // order
    whole = pl.BlockSpec(memory_space=pltpu.VMEM)
    return pl.pallas_call(
        apply_kernel,
        out_shape=jax.ShapeDtypeStruct((blocks * LANES, order), jnp.float32),
        in_specs=[whole, whole],
        out_specs=pl.BlockSpec(memory_space=pl.ANY),
        scratch_shapes=[
            pltpu.VMEM((blocks * LANES, order), jnp.float32),
            pltpu.SemaphoreType.DMA((blocks,)),
        ],
        compiler_params=pltpu.CompilerParams(vmem_limit_bytes=VMEM_LIMIT),
        name="apply",
    )(tiles, inverse)


def shards(snapshots):
    held, length = snapshots.shape
    groups = lax.axis_size("wide")
    tiles = length // LANES
    blocks = snapshots.reshape(held, tiles, LANES).transpose(1, 0, 2)
    blocks = exchange(blocks, "wide").reshape(groups, tiles // groups, held, LANES)
    tiles = blocks.transpose(0, 2, 1, 3).reshape(-1, LANES)
    columns = tiles.reshape(groups * held, length // groups)

    root = math.sqrt(length * lax.axis_size("narrow"))

    inverse, upper, spread = factor(total(gram(columns, 1)), root)

    def rough(state):
        return state[2] > LIMIT

    def again(state):
        inverse, upper, spread = state
        more, next_upper, fresh = factor(total(gram(apply(tiles, inverse), 0)), root)
        fresh = jnp.minimum(fresh, spread / GAIN)
        return product(more, inverse), product(next_upper, upper), fresh

    inverse, upper, _ = lax.while_loop(rough, again, (inverse, upper, spread))
    return apply(tiles, inverse), upper


def solution(mesh):
    in_specs = (P("wide", "narrow"),)
    out_specs = (P(("narrow", "wide"), None), P())
    return jax.shard_map(shards, mesh=mesh, in_specs=in_specs, out_specs=out_specs, check_vma=False)
```
